32 devices in a mesh: groups: 2 (over y), shard: 8 (over z, x), sub: 2 (over core).
Axes of the slice: x: 2, y: 2, z: 4, core: 2. Of those that a mesh axis runs over, the one named last changes fastest.
Arguments:
- query_hidden_states: bfloat16 [384, 32, 4096], P(('groups', 'shard'), None, 'sub'), parts along dimension 0, may hold values from -6 to 6
- passage_hidden_states: bfloat16 [32, 256, 4096], P(('groups', 'shard'), None, 'sub'), parts along dimension 0, may hold values from -6 to 6
- projection_matrix: bfloat16 [4096, 128], P('sub'), may hold values from -0.09375 to 0.09375
- adapter_down_weight: bfloat16 [4096, 16], P('sub'), may hold values from -0.09375 to 0.09375
- adapter_up_weight: bfloat16 [16, 128], replicated, may hold values from -1.5 to 1.5
- passage_pair_index: int32 [384, 9], P(('groups', 'shard')), parts along dimension 0, may hold values from 0 to 15, as said below
- passage_row_table: int32 [32], P('groups'), parts along dimension 0, may hold values from 0 to 15, as said below
Outputs:
- query_loss: float32 [384], P(('groups', 'shard', 'sub')), parts along dimension 0
- grad_down: float32 [8192, 16], P(('groups', 'sub')), parts along dimension 0
- grad_up: float32 [32, 128], P('groups'), parts along dimension 0
The draws below stay inside these ranges and needn't reach their ends.
There are 2 independent parts, one for each index of `groups`. The reference program is written for one: setup_inputs(seed, part) draws one part's arguments, and reference() takes and returns one part's arrays. A program takes and returns all parts, laid end to end along the dimension named above; an argument that names none is the same for every part. Nothing has to cross between parts.
Inputs may be any that keep to these rules, and one draw needn't show every extreme that they name: A permutation: passage id p is stored in row passage_row_table[p] of passage_hidden_states. `passage_pair_index`: query rows form aligned blocks of 12; among the 108 candidates of one block, at most 14 are stored in one owner's rows (rows r with the same r // 2), and in every block some owner holds exactly 14 of them. Candidates of one query may repeat.
All inputs are finite; a program needn't handle non-finite values.
Results may differ from the reference program's by a relative error of at most 0.012.
The reference program's roundings to bfloat16 on the way count: a program that leaves them out, or rounds other values in their place, can miss the bound.
Values may be sent and summed in bfloat16 or wider, within the bound.
No kernel may reach another device: no remote copies, remote signals or barrier semaphores. Data moves between devices by JAX's collectives and lax.ppermute only.
A program may use at most 128 MiB of HBM per device.

```python
import jax
import jax.numpy as jnp
from jax import lax

MODEL_WIDTH = 4096
TOKEN_WIDTH = 128
ADAPTER_RANK = 16
LQ = 32
LP = 256
NEG = 8
QDEV = 24
PDEV = 2
QUERIES = 192
PASSAGES = 16
CAP = 14
N_SUB = 2


def shared_draw(key):
    owners = PASSAGES // PDEV
    table = jax.random.permutation(jax.random.fold_in(key, 101), PASSAGES).astype(jnp.int32)
    inverse = jnp.argsort(table).astype(jnp.int32)
    block_rows = QDEV // N_SUB
    per_block = (1 + NEG) * block_rows
    groups_used = (per_block + CAP - 1) // CAP
    blocks = QUERIES // block_rows
    keys = jax.random.split(jax.random.fold_in(key, 202), blocks)

    def one_block(block_key):
        first, second, third = jax.random.split(block_key, 3)
        chosen = jax.random.permutation(first, owners).astype(jnp.int32)[:groups_used]
        owner = chosen[jnp.arange(per_block) % groups_used]
        owner = jax.random.permutation(second, owner)
        local = jax.random.randint(third, (per_block,), 0, PDEV).astype(jnp.int32)
        return inverse[owner * PDEV + local]
    ids = jax.vmap(one_block)(keys).reshape(QUERIES, 1 + NEG).astype(jnp.int32)
    return (table, ids)


def draw_passage_pair_index(key, part):
    table, ids = shared_draw(key)
    return ids


def draw_passage_row_table(key, part):
    table, ids = shared_draw(key)
    return table


def level_of(own_key, dims, cuts, low, largest):
    def one(axis_at, shards_of):
        draws = jax.random.uniform(jax.random.fold_in(jax.random.fold_in(own_key, 6), axis_at), (shards_of,), jnp.float32, low / len(cuts), largest / len(cuts))
        return jnp.repeat(jnp.exp(draws), dims[axis_at] // shards_of).reshape((-1,) + (1,) * (len(dims) - axis_at - 1))

    level = one(*cuts[0])
    for cut in cuts[1:]:
        level = level * one(*cut)
    return level


def scatter_about(key, dims, width, most, pieces=(), kind=jnp.bfloat16):
    values = width * jax.random.normal(key, dims, jnp.float32)
    if pieces:
        values = values * level_of(key, dims, pieces, -0.22, 0.18)
    return jnp.clip(values, -most, most).astype(kind)


def setup_inputs(seed: int = 0, part: int = 0) -> dict:
    key_of = jax.random.split(jax.random.key(seed), 8)
    own_keys = jax.random.split(jax.random.fold_in(key_of[7], part), 8)
    return {
        "query_hidden_states": scatter_about(own_keys[0], (QUERIES, LQ, MODEL_WIDTH), 1.0, 6.0, ((0, 8), (2, 2))),
        "passage_hidden_states": scatter_about(own_keys[1], (PASSAGES, LP, MODEL_WIDTH), 1.0, 6.0, ((0, 8), (2, 2))),
        "projection_matrix": scatter_about(key_of[2], (MODEL_WIDTH, TOKEN_WIDTH), MODEL_WIDTH ** -0.5, 0.09375, ((0, 2),)),
        "adapter_down_weight": scatter_about(key_of[3], (MODEL_WIDTH, ADAPTER_RANK), MODEL_WIDTH ** -0.5, 0.09375, ((0, 2),)),
        "adapter_up_weight": scatter_about(key_of[4], (ADAPTER_RANK, TOKEN_WIDTH), ADAPTER_RANK ** -0.5, 1.5),
        "passage_pair_index": draw_passage_pair_index(jax.random.fold_in(jax.random.fold_in(key_of[7], part), 71), part),
        "passage_row_table": draw_passage_row_table(jax.random.fold_in(jax.random.fold_in(key_of[7], part), 71), part),
    }


pool_temp = 0.05
loss_temp = 0.05
norm_eps = 1e-06

def embed_tokens(hidden_states, projection_matrix, adapter_down_weight, adapter_up_weight):
    flatten_states = hidden_states.reshape(-1, MODEL_WIDTH)
    frozen_output = jnp.dot(flatten_states, projection_matrix, preferred_element_type=jnp.float32)
    adapter_output = jnp.dot(flatten_states, adapter_down_weight, preferred_element_type=jnp.float32)
    adapter_output_brain = adapter_output.astype(jnp.bfloat16)
    combined_output = frozen_output + jnp.dot(adapter_output_brain, adapter_up_weight, preferred_element_type=jnp.float32)
    factor = lax.rsqrt(lax.optimization_barrier(jnp.sum(combined_output * combined_output, axis=-1, keepdims=True)) + norm_eps)
    return (flatten_states, adapter_output_brain, combined_output, (combined_output * factor).astype(jnp.bfloat16))

def soft_pool(query, bank):
    sims = jnp.einsum('ie,cje->cij', query.astype(jnp.float32), bank, precision=lax.Precision.HIGHEST)
    expo = jnp.exp(sims / pool_temp)
    total = lax.optimization_barrier(jnp.sum(expo, axis=-1))
    weights = (expo / total[..., None]).astype(jnp.bfloat16)
    return (total, weights)

def unnormalize(combined_output, grad):
    factor = lax.rsqrt(lax.optimization_barrier(jnp.sum(combined_output * combined_output, axis=-1, keepdims=True)) + norm_eps)
    inner = lax.optimization_barrier(jnp.sum(combined_output * grad, axis=-1, keepdims=True))
    return factor * grad - factor * factor * factor * inner * combined_output

def reference(query_hidden_states, passage_hidden_states, projection_matrix, adapter_down_weight, adapter_up_weight, passage_pair_index, passage_row_table):
    query_flattened, adapter_query, combined_query, query_token_vectors = embed_tokens(query_hidden_states, projection_matrix, adapter_down_weight, adapter_up_weight)
    passage_flattened, adapter_passage, combined_passage, passage_token_vectors = embed_tokens(passage_hidden_states, projection_matrix, adapter_down_weight, adapter_up_weight)
    vq3 = query_token_vectors.reshape(QUERIES, LQ, TOKEN_WIDTH)
    vp3 = passage_token_vectors.reshape(PASSAGES, LP, TOKEN_WIDTH)
    rows = passage_row_table[passage_pair_index].astype(jnp.int32)

    def forward(item):
        query, row = item
        bank = vp3[row].astype(jnp.float32)
        total, weights = soft_pool(query, bank)
        score = pool_temp * lax.optimization_barrier(jnp.mean(jnp.log(total), axis=1))
        unit = (jnp.einsum('cij,cje->cie', weights.astype(jnp.float32), bank, precision=lax.Precision.HIGHEST) / LQ).astype(jnp.bfloat16)
        return (score, unit)
    scores, units = lax.map(forward, (vq3, rows))
    logits = scores / loss_temp
    summed = lax.optimization_barrier(jnp.sum(jnp.exp(logits), axis=-1))
    query_loss = jnp.log(summed) - logits[:, 0]
    first = (jnp.arange(1 + NEG) == 0).astype(jnp.float32)
    dscore = (jnp.exp(logits) / summed[:, None] - first[None, :]) / loss_temp
    dvq = lax.optimization_barrier(jnp.sum(dscore[:, :, None, None] * units.astype(jnp.float32), axis=1))

    def accumulate(acc, item):
        query, row, grads = item
        bank = vp3[row].astype(jnp.float32)
        total, weights = soft_pool(query, bank)
        gradw = ((grads / LQ)[:, None, None] * weights.astype(jnp.float32)).astype(jnp.bfloat16)
        contrib = jnp.einsum('cij,ie->cje', gradw.astype(jnp.float32), query.astype(jnp.float32), precision=lax.Precision.HIGHEST)
        return (acc.at[row].add(contrib), None)
    dvp, unused = lax.scan(accumulate, jnp.zeros((PASSAGES, LP, TOKEN_WIDTH), jnp.float32), (vq3, rows, dscore))
    dfull_q = unnormalize(combined_query, dvq.reshape(-1, TOKEN_WIDTH))
    dfull_p = unnormalize(combined_passage, dvp.reshape(-1, TOKEN_WIDTH))
    up_weight_float = adapter_up_weight.astype(jnp.float32)
    grad_up = jnp.dot(adapter_query.astype(jnp.float32).T, dfull_q, precision=lax.Precision.HIGHEST)
    grad_up = grad_up + jnp.dot(adapter_passage.astype(jnp.float32).T, dfull_p, precision=lax.Precision.HIGHEST)
    dlow_q = jnp.dot(dfull_q, up_weight_float.T, precision=lax.Precision.HIGHEST).astype(jnp.bfloat16)
    dlow_p = jnp.dot(dfull_p, up_weight_float.T, precision=lax.Precision.HIGHEST).astype(jnp.bfloat16)
    grad_down = jnp.dot(query_flattened.T, dlow_q, preferred_element_type=jnp.float32)
    grad_down = grad_down + jnp.dot(passage_flattened.T, dlow_p, preferred_element_type=jnp.float32)
    return (query_loss, grad_down, grad_up)
```

```python
import functools
import math

import jax
import jax.numpy as jnp
from jax import lax
from jax.experimental import pallas as pl
from jax.experimental.pallas import tpu as pltpu
from jax.sharding import PartitionSpec as P

pool_temp = 0.05
loss_temp = 0.05
norm_eps = 1e-06
bf16 = jnp.bfloat16
f32 = jnp.float32
LANES = 128
EXP_SCALE = math.log2(math.e) / pool_temp
VMEM = pl.BlockSpec(memory_space=pltpu.VMEM)
SMEM = pl.BlockSpec(memory_space=pltpu.SMEM)


def dot(a, b, contract, precision=None):
    return lax.dot_general(
        a, b, ((contract[0], contract[1]), ((), ())), precision=precision, preferred_element_type=f32
    )


NN = ((1,), (0,))
NT = ((1,), (1,))
TN = ((0,), (0,))


def split_dot(exact, wide, contract):
    high = wide.astype(bf16)
    low = (wide - high.astype(f32)).astype(bf16)
    return dot(exact, high, contract) + dot(exact, low, contract)


def project_kernel(core_ref, x_ref, proj_ref, down_ref, send_ref, keep_ref):
    x = x_ref[...]
    base = dot(x, proj_ref[...], NN)
    low = dot(x, down_ref[...], NN)

    def put(ref):
        ref[:, :LANES] = base
        ref[:, LANES:] = low

    pl.when(pl.program_id(0) == 0)(lambda: put(send_ref))
    pl.when(pl.program_id(0) == 1)(lambda: put(keep_ref))


def project(core, rows, projection, down):
    half, width = rows.shape[0] // 2, rows.shape[1]
    shape = jax.ShapeDtypeStruct((half, 2 * LANES), f32)
    return pl.pallas_call(
        project_kernel,
        grid_spec=pltpu.PrefetchScalarGridSpec(
            num_scalar_prefetch=1,
            grid=(2,),
            in_specs=[
                pl.BlockSpec((half, width), lambda j, core: (lax.rem(core[0] + 1 + j, 2), 0)),
                pl.BlockSpec((width, LANES), lambda j, core: (0, 0)),
                pl.BlockSpec((width, LANES), lambda j, core: (0, 0)),
            ],
            out_specs=[
                pl.BlockSpec((half, 2 * LANES), lambda j, core: (0, 0)),
                pl.BlockSpec((half, 2 * LANES), lambda j, core: (0, 0)),
            ],
        ),
        out_shape=(shape, shape),
        name="project",
    )(core, rows, projection, down)


def finish(keep_ref, recv_ref, up):
    rank = up.shape[0]
    low_bf = (keep_ref[:, LANES : LANES + rank] + recv_ref[:, LANES : LANES + rank]).astype(bf16)
    full = keep_ref[:, :LANES] + recv_ref[:, :LANES] + dot(low_bf, up, NN)
    r = lax.rsqrt(jnp.sum(full * full, axis=1, keepdims=True) + norm_eps)
    return low_bf, full * r, r


def pad_lanes(x):
    return jnp.concatenate([x, jnp.zeros((x.shape[0], LANES - x.shape[1]), x.dtype)], axis=1)


def pack_kernel(keep_ref, recv_ref, up_ref, pack_ref, r_ref):
    up = up_ref[...]
    rank, tokens = up.shape[0], keep_ref.shape[0]
    low_bf, vn, r = finish(keep_ref, recv_ref, up)
    pack_ref[:tokens, :] = vn.astype(bf16)
    scaled = jnp.transpose(pad_lanes(low_bf.astype(f32) * r))
    for t in range(tokens // LANES):
        at = tokens + t * rank
        pack_ref[at : at + rank, :] = scaled[:rank, t * LANES : (t + 1) * LANES].astype(bf16)
    r_ref[...] = jnp.transpose(jnp.broadcast_to(r, (tokens, LANES)))[:8, :]


def pack_passage(keep, recv, up):
    tokens, rank = keep.shape[0], up.shape[0]
    return pl.pallas_call(
        pack_kernel,
        in_specs=[VMEM] * 3,
        out_specs=[VMEM] * 2,
        out_shape=(
            jax.ShapeDtypeStruct((tokens + tokens // LANES * rank, LANES), bf16),
            jax.ShapeDtypeStruct((8, tokens), f32),
        ),
        name="pack_passage",
    )(keep, recv, up)


def score_kernel(queries, store, n_packs, *refs):
    packs = refs[:n_packs]
    (owner_ref, keep_ref, recv_ref, up_ref, mult_ref, first_ref) = refs[n_packs : n_packs + 6]
    loss_ref, dlow_q_ref, part_ref, gup_ref = refs[n_packs + 6 : n_packs + 10]
    expo_ref, total_ref, scale_ref, dvq_ref = refs[n_packs + 10 :]
    up = up_ref[...]
    rank = up.shape[0]
    ntok = keep_ref.shape[0]
    qlen = ntok // queries
    plen = part_ref.shape[-1]
    low_bf, vn, r = finish(keep_ref, recv_ref, up)
    vq = vn.astype(bf16)
    vqt = jnp.transpose(vn).astype(bf16)

    def expo_of(pack, p):
        sims = dot(pack[p, :plen, :], vqt, NN)
        return jnp.exp2(sims * EXP_SCALE)

    def over(body):
        at = 0
        for pack in packs:
            n = pack.shape[0]
            if n <= 8:
                for p in range(n):
                    body(pack, p, at + p)
            else:
                lax.fori_loop(0, n, lambda p, c, pack=pack, at=at: (body(pack, p, at + p), c)[1], 0)
            at += n

    def forward(pack, p, pos):
        expo = expo_of(pack, p)
        total_ref[pl.ds(pos, 1), :] = jnp.sum(expo, axis=0, keepdims=True)
        if store:
            expo_ref[pos] = expo.astype(bf16)

    over(forward)

    total = total_ref[...]
    token_query = lax.broadcasted_iota(jnp.int32, (ntok, LANES), 0) // qlen
    same = (token_query == lax.broadcasted_iota(jnp.int32, (ntok, LANES), 1)).astype(f32)
    logits = dot(jnp.log(total), same, NN, lax.Precision.HIGHEST) * (1.0 / qlen)
    mult, first = mult_ref[...], first_ref[...]
    weighted = mult * jnp.exp(logits)
    summed = jnp.sum(weighted, axis=0, keepdims=True)
    live = lax.broadcasted_iota(jnp.int32, summed.shape, 1) < queries
    summed = jnp.where(live, summed, 1.0)
    positive = jnp.sum(first * logits, axis=0, keepdims=True)
    loss_ref[...] = jnp.broadcast_to(jnp.log(summed) - positive, loss_ref.shape)
    dscore = (weighted / summed - first) * (1.0 / loss_temp)
    scale_ref[...] = dot(dscore, same, NT, lax.Precision.HIGHEST) / (total * qlen)

    dvq_ref[...] = jnp.zeros_like(dvq_ref)
    gup_ref[...] = jnp.zeros_like(gup_ref)

    def backward(pack, p, pos):
        vp = pack[p, :plen, :]
        expo = expo_ref[pos].astype(f32) if store else expo_of(pack, p)
        gradw = (expo * scale_ref[pl.ds(pos, 1), :]).astype(bf16)
        dv = dot(gradw, vq, NN)
        dvq_ref[...] += dot(vp, gradw, TN)
        vpf = vp.astype(f32)
        dv = dv - vpf * jnp.sum(vpf * dv, axis=1, keepdims=True)
        part_ref[owner_ref[0, pos], owner_ref[1, pos]] = split_dot(up, dv, NT).astype(bf16)
        for t in range(plen // LANES):
            scaled = pack[p, plen + t * rank : plen + (t + 1) * rank, :]
            gup_ref[...] += split_dot(scaled, dv[t * LANES : (t + 1) * LANES, :], NN)

    over(backward)

    dvq = jnp.transpose(dvq_ref[...])
    dfull = r * (dvq - vn * jnp.sum(vn * dvq, axis=1, keepdims=True))
    dlow_q_ref[...] = split_dot(up, dfull, NT).astype(bf16)
    low_t = jnp.transpose(pad_lanes(low_bf.astype(f32)))[:rank, :].astype(bf16)
    gup_ref[...] += split_dot(low_t, dfull, NN)


def score(packs, owners, keep, recv, up, mult, first, queries, nshard, plen):
    npos, rank, ntok = mult.shape[0], up.shape[0], keep.shape[0]
    store = npos * plen * ntok * 2 <= 12 * 2**20
    return pl.pallas_call(
        functools.partial(score_kernel, queries, store, len(packs)),
        in_specs=[VMEM] * len(packs) + [SMEM] + [VMEM] * 5,
        out_specs=[VMEM] * 4,
        out_shape=(
            jax.ShapeDtypeStruct((8, LANES), f32),
            jax.ShapeDtypeStruct((rank, ntok), bf16),
            jax.ShapeDtypeStruct((nshard, 2, rank, plen), bf16),
            jax.ShapeDtypeStruct((rank, LANES), f32),
        ),
        scratch_shapes=[
            pltpu.VMEM((npos if store else 1, plen, ntok), bf16),
            pltpu.VMEM((npos, ntok), f32),
            pltpu.VMEM((npos, ntok), f32),
            pltpu.VMEM((LANES, ntok), f32),
        ],
        compiler_params=pltpu.CompilerParams(vmem_limit_bytes=48 * 2**20),
        name="score",
    )(*packs, owners, keep, recv, up, mult, first)


def grad_down_kernel(core_ref, x_ref, dlow_ref, out_ref):
    @pl.when(pl.program_id(0) == 0)
    def _():
        out_ref[...] = jnp.zeros_like(out_ref)

    out_ref[...] += dot(dlow_ref[...], x_ref[...], NN)


def grad_down_of(core, rows, mine, other):
    half, width = rows.shape[0] // 2, rows.shape[1]
    rank = mine.shape[0]
    both = jnp.concatenate([mine, other], axis=1)
    return pl.pallas_call(
        grad_down_kernel,
        grid_spec=pltpu.PrefetchScalarGridSpec(
            num_scalar_prefetch=1,
            grid=(2,),
            in_specs=[
                pl.BlockSpec((half, width), lambda j, core: (lax.rem(core[0] + j, 2), 0)),
                pl.BlockSpec((rank, half), lambda j, core: (0, j)),
            ],
            out_specs=pl.BlockSpec((rank, width), lambda j, core: (0, 0)),
        ),
        out_shape=jax.ShapeDtypeStruct((rank, width), f32),
        name="grad_down",
    )(core, rows, both)


def swap(x):
    return lax.ppermute(x, "sub", [(0, 1), (1, 0)])


def across(x, nshard, step):
    return lax.ppermute(x, "shard", [(i, i ^ step) for i in range(nshard)])


def gather_packs(pack, nshard, shard, core):
    if nshard == 8:
        near = jnp.stack([pack] + [across(pack, nshard, k) for k in (2, 4, 6)])
        far = across(near, nshard, 1)
        packs = [near, far, swap(near), swap(far)]
        shards = jnp.bitwise_xor(shard, jnp.array([0, 2, 4, 6, 1, 3, 5, 7], jnp.int32))
    else:
        mine = lax.all_gather(pack, "shard")
        packs = [mine, swap(mine)]
        shards = jnp.arange(nshard, dtype=jnp.int32)
    cores = jnp.repeat(jnp.stack([core, 1 - core]), nshard)
    return packs, jnp.stack([jnp.tile(shards, 2), cores]).astype(jnp.int32)


def sum_over_shards(x, nshard):
    x = x.astype(bf16)
    if nshard != 8:
        return lax.psum(x.astype(f32), "shard")
    x = (x.astype(f32) + across(x, nshard, 1).astype(f32)).astype(bf16)
    a, b, c = (across(x, nshard, k).astype(f32) for k in (2, 4, 6))
    return (x.astype(f32) + a) + (b + c)


def per_device(
    query_hidden_states,
    passage_hidden_states,
    projection_matrix,
    adapter_down_weight,
    adapter_up_weight,
    passage_pair_index,
    passage_row_table,
):
    nshard = lax.axis_size("shard")
    core = lax.axis_index("sub").astype(jnp.int32)
    shard = lax.axis_index("shard").astype(jnp.int32)
    qdev, qlen, width = query_hidden_states.shape
    pdev, plen, _ = passage_hidden_states.shape
    rank = adapter_up_weight.shape[0]
    half = qdev // 2
    core1 = core.reshape(1)
    query_rows = query_hidden_states.reshape(qdev * qlen, width)
    passage_rows = passage_hidden_states.reshape(pdev * plen, width)
    down = jnp.pad(adapter_down_weight, ((0, 0), (0, LANES - rank)))

    send_p, keep_p = project(core1, passage_rows, projection_matrix, down)
    recv_p = swap(send_p)
    send_q, keep_q = project(core1, query_rows, projection_matrix, down)
    recv_q = swap(send_q)
    pack, r_p = pack_passage(keep_p, recv_p, adapter_up_weight)
    packs, owners = gather_packs(pack, nshard, shard, core)

    ids = lax.dynamic_slice_in_dim(passage_pair_index, core * half, half, 0)
    rows = passage_row_table[ids]
    places = owners[0] * pdev + owners[1]
    hits = (places[:, None, None] == rows[None]).astype(f32)
    lanes = ((0, 0), (0, LANES - half))
    mult = jnp.pad(jnp.sum(hits, axis=2), lanes)
    first = jnp.pad(hits[:, :, 0], lanes)

    loss, dlow_q, part, gup = score(
        packs, owners, keep_q, recv_q, adapter_up_weight, mult, first, half, nshard, plen
    )
    query_loss = loss[0, :half]
    parts = lax.all_to_all(part, "shard", split_axis=0, concat_axis=0, tiled=True)
    grad_q = grad_down_of(core1, query_rows, dlow_q, swap(dlow_q))
    gup = gup + swap(gup)
    r_both = jnp.where(core == 0, jnp.stack([r_p, swap(r_p)]), jnp.stack([swap(r_p), r_p]))[:, :1]
    total = jnp.sum(parts.astype(f32), axis=0)
    total = total + swap(total)
    dlow_p = (total * r_both).astype(bf16)
    mine = lax.dynamic_index_in_dim(dlow_p, core, 0, False)
    other = lax.dynamic_index_in_dim(dlow_p, 1 - core, 0, False)
    grad_p = grad_down_of(core1, passage_rows, mine, other)
    summed = sum_over_shards(jnp.concatenate([grad_q + grad_p, gup], axis=1), nshard)
    return (query_loss, jnp.transpose(summed[:, :width]), summed[:, width:])


def solution(mesh):
    placed = (
        P(("groups", "shard"), None, "sub"),
        P(("groups", "shard"), None, "sub"),
        P("sub", None),
        P("sub", None),
        P(),
        P(("groups", "shard"), None),
        P("groups"),
    )
    return jax.shard_map(
        per_device,
        mesh=mesh,
        in_specs=placed,
        out_specs=(P(("groups", "shard", "sub")), P(("groups", "sub"), None), P("groups", None)),
        check_vma=False,
    )
```

```python
import functools
import math

import jax
import jax.numpy as jnp
from jax import lax
from jax.experimental import pallas as pl
from jax.experimental.pallas import tpu as pltpu
from jax.sharding import PartitionSpec as P

pool_temp = 0.05
loss_temp = 0.05
norm_eps = 1e-06
bf16 = jnp.bfloat16
f32 = jnp.float32
LANES = 128
EXP_SCALE = math.log2(math.e) / pool_temp
VMEM = pl.BlockSpec(memory_space=pltpu.VMEM)
SMEM = pl.BlockSpec(memory_space=pltpu.SMEM)
HBM = pl.BlockSpec(memory_space=pltpu.HBM)


def dot(a, b, contract, precision=None):
    return lax.dot_general(
        a, b, ((contract[0], contract[1]), ((), ())), precision=precision, preferred_element_type=f32
    )


NN = ((1,), (0,))
NT = ((1,), (1,))
TN = ((0,), (0,))


def project_kernel(info_ref, p_hbm, q_hbm, proj_hbm, down_hbm, send_ref, keep_ref, x_ref, weight_ref, down_ref, sems):
    core = info_ref[2]
    weights = [
        pltpu.make_async_copy(down_hbm, down_ref, sems.at[0]),
        pltpu.make_async_copy(proj_hbm, weight_ref.at[:, :LANES], sems.at[1]),
    ]
    loads = []
    for i, (owner, out) in enumerate(((1 - core, send_ref), (core, keep_ref))):
        at = 0
        for j, source in enumerate((p_hbm, q_hbm)):
            half = source.shape[0] // 2
            rows = pl.ds(pl.multiple_of(owner * half, LANES), half)
            to = slice(at, at + half)
            copy = pltpu.make_async_copy(source.at[rows, :], x_ref.at[i, to, :], sems.at[2 + 2 * i + j])
            loads.append((copy, out, i, to))
            at += half
    for copy in weights:
        copy.start()
    for copy, _, _, _ in loads[:2]:
        copy.start()
    weights[0].wait()
    rank, width = down_ref.shape
    low = jnp.concatenate([down_ref[...].astype(f32), jnp.zeros((LANES - rank, width), f32)], axis=0)
    weight_ref[:, LANES:] = jnp.transpose(low).astype(bf16)
    weights[1].wait()
    for copy, _, _, _ in loads[2:]:
        copy.start()
    for copy, out, i, to in loads:
        copy.wait()
        out[to, :] = dot(x_ref[i, to, :], weight_ref[...], NN)


def project(info, passage_rows, query_rows, projection, down):
    half, width = (passage_rows.shape[0] + query_rows.shape[0]) // 2, query_rows.shape[1]
    rank = down.shape[0]
    shape = jax.ShapeDtypeStruct((half, 2 * LANES), f32)
    operands = (passage_rows, query_rows, projection, down)
    operands = [pltpu.with_memory_space_constraint(x, pltpu.HBM) for x in operands]
    return pl.pallas_call(
        project_kernel,
        in_specs=[SMEM] + [HBM] * 4,
        out_specs=[VMEM] * 2,
        out_shape=(shape, shape),
        scratch_shapes=[
            pltpu.VMEM((2, half, width), bf16),
            pltpu.VMEM((width, 2 * LANES), bf16),
            pltpu.VMEM((rank, width), bf16),
            pltpu.SemaphoreType.DMA((6,)),
        ],
        compiler_params=pltpu.CompilerParams(vmem_limit_bytes=12 * 2**20),
        name="project",
    )(info, *operands)


def finish(keep, recv, up):
    rank = up.shape[0]
    low_bf = (keep[:, LANES : LANES + rank] + recv[:, LANES : LANES + rank]).astype(bf16)
    full = keep[:, :LANES] + recv[:, :LANES] + dot(low_bf, up, NN)
    r = lax.rsqrt(jnp.sum(full * full, axis=1, keepdims=True) + norm_eps)
    return low_bf, full * r, r


def pad_lanes(x):
    return jnp.concatenate([x, jnp.zeros((x.shape[0], LANES - x.shape[1]), x.dtype)], axis=1)


def pack_kernel(sizes, info_ref, table_ref, ids_ref, keep_ref, recv_ref, up_ref, p_ref, q_ref, r_ref):
    up = up_ref[...]
    rank = up.shape[0]
    low_bf, vn, r = finish(keep_ref[...], recv_ref[...], up)
    scaled = jnp.transpose(pad_lanes(low_bf.astype(f32) * r))[:rank, :].astype(bf16)
    vn = vn.astype(bf16)
    start = 0
    for ref, tokens in zip((p_ref, q_ref), sizes, strict=True):
        ref[:tokens, :] = vn[start : start + tokens, :]
        for t in range(tokens // LANES):
            at = start + t * LANES
            ref[tokens + t * rank : tokens + (t + 1) * rank, :] = scaled[:, at : at + LANES]
        start += tokens
    r_ref[...] = jnp.transpose(jnp.broadcast_to(r, (start, LANES)))[:8, :]
    ids = ids_ref[...]
    cands, qdev = ids.shape
    n_ids = table_ref.shape[0]
    if n_ids <= 16:
        rows = jnp.zeros(ids.shape, jnp.int32)
        for i in range(n_ids):
            rows = jnp.where(ids == i, table_ref[i], rows)
    else:
        rows = lax.fori_loop(
            0, n_ids, lambda i, c: jnp.where(ids == i, table_ref[i], c), jnp.zeros(ids.shape, jnp.int32)
        )
    half = qdev // 2
    wide = jnp.concatenate([pad_lanes(rows.astype(f32)), jnp.full((16 - cands, LANES), -1.0, f32)], axis=0)
    place = info_ref[0] * half
    wide = pltpu.roll(wide, lax.rem(place - info_ref[2] * half + LANES, LANES), 1)
    lane = lax.broadcasted_iota(jnp.int32, wide.shape, 1)
    wide = jnp.where((lane >= place) & (lane < place + half), wide, -1.0)
    q_ref[q_ref.shape[0] - 16 :, :] = wide.astype(bf16)


def pack_tokens(info, table, ids, keep, recv, up, ptok, qtok):
    rank = up.shape[0]
    return pl.pallas_call(
        functools.partial(pack_kernel, (ptok, qtok)),
        in_specs=[SMEM] * 2 + [VMEM] * 4,
        out_specs=[VMEM] * 3,
        out_shape=(
            jax.ShapeDtypeStruct((ptok + ptok // LANES * rank, LANES), bf16),
            jax.ShapeDtypeStruct((qtok + qtok // LANES * rank + 16, LANES), bf16),
            jax.ShapeDtypeStruct((8, ptok + qtok), f32),
        ),
        compiler_params=pltpu.CompilerParams(vmem_limit_bytes=8 * 2**20),
        name="pack_tokens",
    )(info, table, ids, keep, recv, up)


def both_queries(lo, mine_ref, other_ref, at):
    mine, other = mine_ref[at, :], other_ref[at, :]
    return jnp.where(lo == 0, mine, other), jnp.where(lo == 0, other, mine)


def over_packs(packs, body):
    at = 0
    for pack in packs:
        n = pack.shape[0]
        if n <= 8:
            for p in range(n):
                body(pack, p, at + p)
        else:
            lax.fori_loop(0, n, lambda p, c, pack=pack, at=at: (body(pack, p, at + p), c)[1], 0)
        at += n


def same_query(shape, dim, qlen):
    token = lax.broadcasted_iota(jnp.int32, shape, dim) // qlen
    return (token == lax.broadcasted_iota(jnp.int32, shape, 1 - dim)).astype(bf16)


def parts_of(wide, n):
    parts = []
    for _ in range(n):
        parts.append(wide.astype(bf16))
        wide = wide - parts[-1].astype(f32)
    return parts


def expo_of(vp, vqt):
    return jnp.exp2(dot(vp, vqt, NN) * EXP_SCALE)


def forward_kernel(cfg, *refs):
    qlen, qtok, plen, store, where, n_packs = cfg
    packs = refs[:n_packs]
    info_ref, mine_ref, other_ref = refs[n_packs : n_packs + 3]
    stats_ref, total_ref, sums_ref, expo_ref, vqt_ref = refs[n_packs + 3 :]
    lo = info_ref[0]
    first_half, second_half = both_queries(lo, mine_ref, other_ref, slice(0, qtok))
    vqt_ref[:, :qtok] = jnp.transpose(first_half.astype(f32)).astype(bf16)
    vqt_ref[:, qtok:] = jnp.transpose(second_half.astype(f32)).astype(bf16)
    tail = slice(mine_ref.shape[0] - 16, mine_ref.shape[0])
    rows = jnp.maximum(mine_ref[tail, :].astype(f32), other_ref[tail, :].astype(f32))

    def forward(pack, p, pos):
        expo = expo_of(pack[p, :plen, :], vqt_ref[...])
        total_ref[pl.ds(pos, 1), :] = jnp.sum(expo, axis=0, keepdims=True)
        if store:
            expo_ref[pos] = expo.astype(bf16)
        hi, core = where(info_ref, pos)
        here = (rows == ((hi * 2 + lo) * 2 + core).astype(f32)).astype(f32)
        stats_ref[1, pl.ds(pos, 1), :] = jnp.sum(here, axis=0, keepdims=True)
        stats_ref[2, pl.ds(pos, 1), :] = here[:1, :]

    over_packs(packs, forward)
    same = same_query((2 * qtok, LANES), 0, qlen)
    logits = sum(dot(part, same, NN) for part in parts_of(jnp.log(total_ref[...]), 3)) * (1.0 / qlen)
    stats_ref[0] = logits
    sums_ref[...] = jnp.zeros_like(sums_ref)
    sums_ref[:1, :] = jnp.sum(stats_ref[1] * jnp.exp(logits), axis=0, keepdims=True)
    sums_ref[1:2, :] = jnp.sum(stats_ref[2] * logits, axis=0, keepdims=True)


def backward_kernel(cfg, *refs):
    qlen, qtok, plen, store, where, n_packs = cfg
    packs = refs[:n_packs]
    info_ref, mine_ref, other_ref, up_ref, stats_ref, total_ref, sums_ref, recv_ref, expo_ref, vqt_ref = refs[
        n_packs : n_packs + 10
    ]
    refs = refs[n_packs + 10 :]
    n_parts = n_packs // 2 if store else 1
    part_refs, (dmine_ref, dother_ref, gup_ref, loss_ref) = refs[:n_parts], refs[n_parts : n_parts + 4]
    scale_ref, dvqt_ref, grad_ref, dv_ref, dvb_ref = refs[n_parts + 4 :]
    up = up_ref[...]
    rank = up.shape[0]
    lo = info_ref[0]
    vq = jnp.concatenate(both_queries(lo, mine_ref, other_ref, slice(0, qtok)), axis=0)
    logits, mult, first = stats_ref[0], stats_ref[1], stats_ref[2]
    summed = sums_ref[:1, :] + recv_ref[:1, :]
    live = lax.broadcasted_iota(jnp.int32, summed.shape, 1) < 2 * qtok // qlen
    summed = jnp.where(live, summed, 1.0)
    loss_ref[...] = jnp.broadcast_to(jnp.log(summed) - (sums_ref[1:2, :] + recv_ref[1:2, :]), loss_ref.shape)
    dscore = (mult * jnp.exp(logits) / summed - first) * (1.0 / loss_temp)
    same = same_query((LANES, 2 * qtok), 1, qlen)
    scale_ref[...] = sum(dot(part, same, NN) for part in parts_of(dscore, 2)) / (total_ref[...] * qlen)

    def scaled_low(pack, p):
        blocks = range(plen, plen + plen // LANES * rank, rank)
        return jnp.concatenate([pack[p, at : at + rank, :] for at in blocks], axis=1)

    def project_out(vp, dv):
        vpf = vp.astype(f32)
        return (dv - vpf * jnp.sum(vpf * dv, axis=1, keepdims=True)).astype(bf16)

    if store:
        for pos in range(n_packs):
            rows = slice(pos * plen, (pos + 1) * plen)
            grad_ref[rows, :] = (expo_ref[pos].astype(f32) * scale_ref[pos : pos + 1, :]).astype(bf16)
        dv_ref[...] = dot(grad_ref[...], vq, NN)
        for pos, pack in enumerate(packs):
            rows = slice(pos * plen, (pos + 1) * plen)
            vp = pack[0, :plen, :]
            dvqt = dot(vp, grad_ref[rows, :], TN)
            dvqt_ref[...] = dvqt if pos == 0 else dvqt_ref[...] + dvqt
            dv = project_out(vp, dv_ref[rows, :])
            dvb_ref[rows, :] = dv
            part_refs[pos % n_parts][where(info_ref, pos)[1]] = dot(up, dv, NT).astype(bf16)
        lows = jnp.concatenate([scaled_low(pack, 0) for pack in packs], axis=1)
        gup = dot(lows, dvb_ref[...], NN)
    else:
        dvqt_ref[...] = jnp.zeros_like(dvqt_ref)
        gup_ref[...] = jnp.zeros_like(gup_ref)

        def backward(pack, p, pos):
            vp = pack[p, :plen, :]
            grad = (expo_of(vp, vqt_ref[...]) * scale_ref[pl.ds(pos, 1), :]).astype(bf16)
            dvqt_ref[...] += dot(vp, grad, TN)
            dv = project_out(vp, dot(grad, vq, NN))
            hi, core = where(info_ref, pos)
            part_refs[0][hi, core] = dot(up, dv, NT).astype(bf16)
            gup_ref[...] += dot(scaled_low(pack, p), dv, NN)

        over_packs(packs, backward)
        gup = gup_ref[...]

    vqt = vqt_ref[...].astype(f32)
    dvqt = dvqt_ref[...]
    dvqt = (dvqt - vqt * jnp.sum(vqt * dvqt, axis=0, keepdims=True)).astype(bf16)
    dlow = dot(up, dvqt, NN)
    dmine_ref[...] = jnp.where(lo == 0, dlow[:, :qtok], dlow[:, qtok:])
    dother_ref[...] = jnp.where(lo == 0, dlow[:, qtok:], dlow[:, :qtok])
    lows = [
        both_queries(lo, mine_ref, other_ref, slice(at, at + rank))
        for at in range(qtok, qtok + qtok // LANES * rank, rank)
    ]
    lows = jnp.concatenate([low[0] for low in lows] + [low[1] for low in lows], axis=1)
    gup_ref[...] = gup + dot(lows, dvqt, NT)


def places(steps):
    def where(info_ref, pos):
        n = len(steps)
        if n <= 8:
            return jnp.bitwise_xor(info_ref[1], steps[pos % n]), info_ref[2] if pos < n else 1 - info_ref[2]
        return lax.rem(pos, n), jnp.where(pos < n, info_ref[2], 1 - info_ref[2])

    return where


def score_forward(packs, steps, info, mine, other, qlen, qtok, plen):
    npos = 2 * len(steps)
    store = len(packs) == npos
    cfg = (qlen, qtok, plen, store, places(steps), len(packs))
    return pl.pallas_call(
        functools.partial(forward_kernel, cfg),
        in_specs=[VMEM] * len(packs) + [SMEM] + [VMEM] * 2,
        out_specs=[VMEM] * 5,
        out_shape=(
            jax.ShapeDtypeStruct((3, npos, LANES), f32),
            jax.ShapeDtypeStruct((npos, 2 * qtok), f32),
            jax.ShapeDtypeStruct((8, LANES), f32),
            jax.ShapeDtypeStruct((npos, plen, 2 * qtok) if store else (1, 16, LANES), bf16),
            jax.ShapeDtypeStruct((LANES, 2 * qtok), bf16),
        ),
        compiler_params=pltpu.CompilerParams(vmem_limit_bytes=(16 if store else 40) * 2**20),
        name="score_forward",
    )(*packs, info, mine, other)


def score_backward(packs, steps, info, mine, other, up, stats, total, sums, recv, expo, vqt, qlen, qtok, plen):
    npos, rank = 2 * len(steps), up.shape[0]
    store = len(packs) == npos
    cfg = (qlen, qtok, plen, store, places(steps), len(packs))
    part = jax.ShapeDtypeStruct((2, rank, plen), bf16)
    whole = jax.ShapeDtypeStruct((len(steps), 2, rank, plen), bf16)
    kept = npos * plen if store else 16
    parts = (part,) * len(steps) if store else (whole,)
    return pl.pallas_call(
        functools.partial(backward_kernel, cfg),
        in_specs=[VMEM] * len(packs) + [SMEM] + [VMEM] * 9,
        out_specs=[VMEM] * (len(parts) + 4),
        out_shape=(
            *parts,
            jax.ShapeDtypeStruct((rank, qtok), f32),
            jax.ShapeDtypeStruct((rank, qtok), f32),
            jax.ShapeDtypeStruct((rank, LANES), f32),
            jax.ShapeDtypeStruct((8, LANES), f32),
        ),
        scratch_shapes=[
            pltpu.VMEM((npos, 2 * qtok), f32),
            pltpu.VMEM((LANES, 2 * qtok), f32),
            pltpu.VMEM((kept, 2 * qtok), bf16),
            pltpu.VMEM((kept, LANES), f32),
            pltpu.VMEM((kept, LANES), bf16),
        ],
        compiler_params=pltpu.CompilerParams(vmem_limit_bytes=(20 if store else 40) * 2**20),
        name="score_backward",
    )(*packs, info, mine, other, up, stats, total, sums, recv, expo, vqt)


def collect_kernel(n, *refs):
    parts, (mine_ref, recv_ref, r_ref, up_ref, out_ref) = refs[:n], refs[n:]
    _, _, plen = parts[0].shape
    qtok = mine_ref.shape[1]
    for i in range(2):
        out_ref[:, i * plen : (i + 1) * plen] = sum(part[i].astype(f32) for part in parts)
    out_ref[:, 2 * plen : 2 * plen + qtok] = (mine_ref[...] + recv_ref[...]) * r_ref[:1, plen:]
    out_ref[:, 2 * plen + qtok :] = up_ref[...]


def collect(parts, mine, recv, r, up):
    rank, qtok = mine.shape
    plen = parts[0].shape[2]
    return pl.pallas_call(
        functools.partial(collect_kernel, len(parts)),
        in_specs=[VMEM] * (len(parts) + 4),
        out_specs=VMEM,
        out_shape=jax.ShapeDtypeStruct((rank, 2 * plen + qtok + LANES), f32),
        compiler_params=pltpu.CompilerParams(vmem_limit_bytes=4 * 2**20),
        name="collect",
    )(*parts, mine, recv, r, up)


def grad_kernel(plen, qtok, info_ref, p_ref, q_ref, mine_ref, other_ref, r_mine_ref, r_other_ref, out_ref):
    core = info_ref[2]
    width = p_ref.shape[1]
    queries = slice(2 * plen, 2 * plen + qtok)
    q_mine, q_other = mine_ref[:, queries].astype(bf16), other_ref[:, queries].astype(bf16)
    q_dlow = [jnp.where(core == i, q_mine, q_other) for i in range(2)]
    p_dlow = []
    for i in range(2):
        r = jnp.where(core == i, r_mine_ref[:1, :plen], r_other_ref[:1, :plen])
        rows = slice(i * plen, (i + 1) * plen)
        p_dlow.append(((mine_ref[:, rows] + other_ref[:, rows]) * r).astype(bf16))
    total = dot(jnp.concatenate(q_dlow, axis=1), q_ref[...], NN)
    total += dot(jnp.concatenate(p_dlow, axis=1), p_ref[...], NN)
    out_ref[:, :width] = total.astype(bf16)
    out_ref[:, width:] = (mine_ref[:, 2 * plen + qtok :] + other_ref[:, 2 * plen + qtok :]).astype(bf16)


def grad_all(info, passage_rows, query_rows, mine, other, r_mine, r_other, plen, qtok):
    rank, width = mine.shape[0], passage_rows.shape[1]
    return pl.pallas_call(
        functools.partial(grad_kernel, plen, qtok),
        in_specs=[SMEM] + [VMEM] * 6,
        out_specs=VMEM,
        out_shape=jax.ShapeDtypeStruct((rank, width + LANES), bf16),
        compiler_params=pltpu.CompilerParams(vmem_limit_bytes=4 * 2**20),
        name="grad_all",
    )(info, passage_rows, query_rows, mine, other, r_mine, r_other)


def add_kernel(a_ref, b_ref, c_ref, d_ref, down_ref, up_ref):
    total = (a_ref[...].astype(f32) + b_ref[...].astype(f32)) + (
        c_ref[...].astype(f32) + d_ref[...].astype(f32)
    )
    width = down_ref.shape[1]
    down_ref[...] = total[:, :width]
    up_ref[...] = total[:, width:]


def add_four(parts, width):
    rank = parts[0].shape[0]
    return pl.pallas_call(
        add_kernel,
        in_specs=[VMEM] * 4,
        out_specs=[VMEM] * 2,
        out_shape=(
            jax.ShapeDtypeStruct((rank, width), f32),
            jax.ShapeDtypeStruct((rank, LANES), f32),
        ),
        compiler_params=pltpu.CompilerParams(vmem_limit_bytes=4 * 2**20),
        name="add_four",
    )(*parts)


def swap(x):
    return lax.ppermute(x, "sub", [(0, 1), (1, 0)])


def across(x, nshard, step):
    return lax.ppermute(x, "shard", [(i, i ^ step) for i in range(nshard)])


def gather_packs(pack, nshard, groups):
    if nshard == 8:
        pack = pack[None]
        near = [pack] + [across(pack, nshard, k) for k in (6, 4, 2)]
        return near + [swap(piece) for piece in near], (0, 3, 2, 1)
    near = lax.all_gather(pack, "shard", axis_index_groups=groups)
    return [near, swap(near)], tuple(range(nshard // 2))


def exchange_parts(parts, steps, nshard, groups):
    if len(parts) == 1:
        parts = lax.all_to_all(parts[0], "shard", split_axis=0, concat_axis=0, tiled=True, axis_index_groups=groups)
        return [jnp.sum(parts.astype(f32), axis=0)]
    return [parts[0]] + [across(part, nshard, 2 * step) for part, step in zip(parts[1:], steps[1:], strict=True)]


def sum_over_shards(x, nshard, width):
    if nshard != 8:
        x = lax.psum(x.astype(f32), "shard")
        return x[:, :width], x[:, width:]
    x = (x.astype(f32) + across(x, nshard, 1).astype(f32)).astype(bf16)
    return add_four([x] + [across(x, nshard, k) for k in (2, 4, 6)], width)


def per_device(
    query_hidden_states,
    passage_hidden_states,
    projection_matrix,
    adapter_down_weight,
    adapter_up_weight,
    passage_pair_index,
    passage_row_table,
):
    nshard = lax.axis_size("shard")
    core = lax.axis_index("sub").astype(jnp.int32)
    shard = lax.axis_index("shard").astype(jnp.int32)
    info = jnp.stack([shard % 2, shard // 2, core])
    groups = [list(range(parity, nshard, 2)) for parity in range(2)]
    qdev, qlen, width = query_hidden_states.shape
    pdev, plen, _ = passage_hidden_states.shape
    half = qdev // 2
    qtok = half * qlen
    query_rows = query_hidden_states.reshape(qdev * qlen, width)
    passage_rows = passage_hidden_states.reshape(pdev * plen, width)

    send, keep = project(info, passage_rows, query_rows, projection_matrix, jnp.transpose(adapter_down_weight))
    ppack, mine, r = pack_tokens(
        info, passage_row_table, jnp.transpose(passage_pair_index), keep, swap(send), adapter_up_weight, plen, qtok
    )
    other = across(mine, nshard, 1)
    packs, steps = gather_packs(ppack, nshard, groups)
    r_other = swap(r)

    stats, total, sums, expo, vqt = score_forward(packs, steps, info, mine, other, qlen, qtok, plen)
    *parts, dlow_mine, dlow_other, gup, loss = score_backward(
        packs,
        steps,
        info,
        mine,
        other,
        adapter_up_weight,
        stats,
        total,
        sums,
        across(sums, nshard, 1),
        expo,
        vqt,
        qlen,
        qtok,
        plen,
    )
    parts = exchange_parts(parts, steps, nshard, groups)
    collected = collect(parts, dlow_mine, across(dlow_other, nshard, 1), r, gup)
    grads = grad_all(info, passage_rows, query_rows, collected, swap(collected), r, r_other, plen, qtok)
    query_loss = lax.dynamic_slice_in_dim(loss[0], info[0] * half, half, 0)
    down_sum, up_sum = sum_over_shards(grads, nshard, width)
    return (query_loss, jnp.transpose(down_sum), up_sum)


def solution(mesh):
    placed = (
        P(("groups", "shard"), None, "sub"),
        P(("groups", "shard"), None, "sub"),
        P("sub", None),
        P("sub", None),
        P(),
        P(("groups", "shard"), None),
        P("groups"),
    )
    return jax.shard_map(
        per_device,
        mesh=mesh,
        in_specs=placed,
        out_specs=(P(("groups", "shard", "sub")), P(("groups", "sub"), None), P("groups", None)),
        check_vma=False,
    )
```

```python
import functools
import math

import jax
import jax.numpy as jnp
from jax import lax
from jax.experimental import pallas as pl
from jax.experimental.pallas import tpu as pltpu
from jax.sharding import PartitionSpec as P

pool_temp = 0.05
loss_temp = 0.05
norm_eps = 1e-06
bf16 = jnp.bfloat16
f32 = jnp.float32
LANES = 128
EXP_SCALE = math.log2(math.e) / pool_temp
VMEM = pl.BlockSpec(memory_space=pltpu.VMEM)
SMEM = pl.BlockSpec(memory_space=pltpu.SMEM)
HBM = pl.BlockSpec(memory_space=pltpu.HBM)


def cost(microseconds):
    return pl.CostEstimate(
        flops=int(microseconds * 1.1e9), bytes_accessed=int(microseconds * 3.5e6), transcendentals=0
    )


def dot(a, b, contract, precision=None):
    return lax.dot_general(
        a, b, ((contract[0], contract[1]), ((), ())), precision=precision, preferred_element_type=f32
    )


NN = ((1,), (0,))
NT = ((1,), (1,))
TN = ((0,), (0,))


def put_projection(out_ref, projected, rank):
    tokens = projected.shape[0]
    out_ref[:tokens, :] = projected[:, :LANES]
    low = jnp.transpose(projected[:, LANES:])[:rank, :]
    for t in range(tokens // LANES):
        out_ref[tokens + t * rank : tokens + (t + 1) * rank, :] = low[:, t * LANES : (t + 1) * LANES]


def project_passages_kernel(
    info_ref, p_hbm, q_hbm, proj_hbm, down_hbm, send_ref, keep_ref, q_ref, weight_ref, p_ref, down_ref, sems
):
    core = info_ref[2]
    half = p_hbm.shape[0] // 2
    weights = [
        pltpu.make_async_copy(down_hbm, down_ref, sems.at[0]),
        pltpu.make_async_copy(proj_hbm, weight_ref.at[:, :LANES], sems.at[1]),
    ]
    loads = []
    for i, owner in enumerate((1 - core, core)):
        rows = pl.ds(pl.multiple_of(owner * half, LANES), half)
        loads.append(pltpu.make_async_copy(p_hbm.at[rows, :], p_ref.at[i], sems.at[2 + i]))
    queries = pltpu.make_async_copy(q_hbm, q_ref, sems.at[4])
    for copy in weights + loads:
        copy.start()
    weights[0].wait()
    rank, width = down_ref.shape
    low = jnp.concatenate([down_ref[...].astype(f32), jnp.zeros((LANES - rank, width), f32)], axis=0)
    weight_ref[:, LANES:] = jnp.transpose(low).astype(bf16)
    weights[1].wait()
    queries.start()
    for i, out in enumerate((send_ref, keep_ref)):
        loads[i].wait()
        put_projection(out, dot(p_ref[i], weight_ref[...], NN), rank)
    queries.wait()


def project_passages(info, passage_rows, query_rows, projection, down):
    half, width = passage_rows.shape[0] // 2, passage_rows.shape[1]
    rank = down.shape[0]
    shape = jax.ShapeDtypeStruct((half + half // LANES * rank, LANES), f32)
    operands = (passage_rows, query_rows, projection, down)
    operands = [pltpu.with_memory_space_constraint(x, pltpu.HBM) for x in operands]
    return pl.pallas_call(
        project_passages_kernel,
        in_specs=[SMEM] + [HBM] * 4,
        out_specs=[VMEM] * 4,
        out_shape=(
            shape,
            shape,
            pltpu.VMEM(query_rows.shape, bf16),
            pltpu.VMEM((width, 2 * LANES), bf16),
        ),
        scratch_shapes=[
            pltpu.VMEM((2, half, width), bf16),
            pltpu.VMEM((rank, width), bf16),
            pltpu.SemaphoreType.DMA((5,)),
        ],
        compiler_params=pltpu.CompilerParams(vmem_limit_bytes=8 * 2**20),
        cost_estimate=cost(3.7),
        name="project_passages",
    )(info, *operands)


def project_queries_kernel(rank, info_ref, q_ref, weight_ref, send_ref, keep_ref):
    half = q_ref.shape[0] // 2
    for owner, out in ((1 - info_ref[2], send_ref), (info_ref[2], keep_ref)):
        rows = pl.ds(pl.multiple_of(owner * half, LANES), half)
        put_projection(out, dot(q_ref[rows, :], weight_ref[...], NN), rank)


def project_queries(info, query_rows, weight, rank):
    half = query_rows.shape[0] // 2
    shape = jax.ShapeDtypeStruct((half + half // LANES * rank, LANES), f32)
    return pl.pallas_call(
        functools.partial(project_queries_kernel, rank),
        in_specs=[SMEM] + [VMEM] * 2,
        out_specs=[VMEM] * 2,
        out_shape=(shape, shape),
        compiler_params=pltpu.CompilerParams(vmem_limit_bytes=4 * 2**20),
        cost_estimate=cost(1.5),
        name="project_queries",
    )(info, query_rows, weight)


def pad_lanes(x):
    return jnp.concatenate([x, jnp.zeros((x.shape[0], LANES - x.shape[1]), x.dtype)], axis=1)


def pack_rows(keep_ref, recv_ref, up, out_ref, r_ref):
    rank, tokens = up.shape[0], r_ref.shape[1]
    for t in range(tokens // LANES):
        block = slice(t * LANES, (t + 1) * LANES)
        rows = slice(tokens + t * rank, tokens + (t + 1) * rank)
        low = (keep_ref[rows, :] + recv_ref[rows, :]).astype(bf16)
        full = keep_ref[block, :] + recv_ref[block, :] + dot(low, up, TN)
        r = lax.rsqrt(jnp.sum(full * full, axis=1, keepdims=True) + norm_eps)
        out_ref[block, :] = (full * r).astype(bf16)
        r = jnp.transpose(jnp.broadcast_to(r, (LANES, LANES)))
        out_ref[rows, :] = (low.astype(f32) * r[:rank, :]).astype(bf16)
        r_ref[:, block] = r[:8, :]


def pack_passage_kernel(keep_ref, recv_ref, up_ref, out_ref, r_ref):
    pack_rows(keep_ref, recv_ref, up_ref[...], out_ref, r_ref)


def pack_passage(keep, recv, up):
    rank = up.shape[0]
    tokens = keep.shape[0] // (LANES + rank) * LANES
    return pl.pallas_call(
        pack_passage_kernel,
        in_specs=[VMEM] * 3,
        out_specs=[VMEM] * 2,
        out_shape=(
            jax.ShapeDtypeStruct((tokens + tokens // LANES * rank, LANES), bf16),
            jax.ShapeDtypeStruct((8, tokens), f32),
        ),
        compiler_params=pltpu.CompilerParams(vmem_limit_bytes=4 * 2**20),
        cost_estimate=cost(6),
        name="pack_passage",
    )(keep, recv, up)


def pack_queries_kernel(info_ref, table_ref, ids_ref, keep_ref, recv_ref, up_ref, out_ref, r_ref):
    pack_rows(keep_ref, recv_ref, up_ref[...], out_ref, r_ref)
    ids = ids_ref[...]
    cands, qdev = ids.shape
    n_ids = table_ref.shape[0]
    if n_ids <= 16:
        rows = jnp.zeros(ids.shape, jnp.int32)
        for i in range(n_ids):
            rows = jnp.where(ids == i, table_ref[i], rows)
    else:
        rows = lax.fori_loop(
            0, n_ids, lambda i, c: jnp.where(ids == i, table_ref[i], c), jnp.zeros(ids.shape, jnp.int32)
        )
    half = qdev // 2
    wide = jnp.concatenate([pad_lanes(rows.astype(f32)), jnp.full((16 - cands, LANES), -1.0, f32)], axis=0)
    place = info_ref[0] * half
    wide = pltpu.roll(wide, lax.rem(place - info_ref[2] * half + LANES, LANES), 1)
    lane = lax.broadcasted_iota(jnp.int32, wide.shape, 1)
    wide = jnp.where((lane >= place) & (lane < place + half), wide, -1.0)
    out_ref[out_ref.shape[0] - 16 :, :] = wide.astype(bf16)


def pack_queries(info, table, ids, keep, recv, up):
    rank = up.shape[0]
    tokens = keep.shape[0] // (LANES + rank) * LANES
    return pl.pallas_call(
        pack_queries_kernel,
        in_specs=[SMEM] * 2 + [VMEM] * 4,
        out_specs=[VMEM] * 2,
        out_shape=(
            jax.ShapeDtypeStruct((tokens + tokens // LANES * rank + 16, LANES), bf16),
            jax.ShapeDtypeStruct((8, tokens), f32),
        ),
        compiler_params=pltpu.CompilerParams(vmem_limit_bytes=4 * 2**20),
        cost_estimate=cost(0.9),
        name="pack_queries",
    )(info, table, ids, keep, recv, up)


def both_queries(lo, mine_ref, other_ref, at):
    mine, other = mine_ref[at, :], other_ref[at, :]
    return jnp.where(lo == 0, mine, other), jnp.where(lo == 0, other, mine)


def over_packs(packs, body):
    at = 0
    for pack in packs:
        n = pack.shape[0]
        if n <= 8:
            for p in range(n):
                body(pack, p, at + p)
        else:
            lax.fori_loop(0, n, lambda p, c, pack=pack, at=at: (body(pack, p, at + p), c)[1], 0)
        at += n


def same_query(shape, dim, qlen):
    token = lax.broadcasted_iota(jnp.int32, shape, dim) // qlen
    return (token == lax.broadcasted_iota(jnp.int32, shape, 1 - dim)).astype(bf16)


def parts_of(wide, n):
    parts = []
    for _ in range(n):
        parts.append(wide.astype(bf16))
        wide = wide - parts[-1].astype(f32)
    return parts


def expo_of(vp, vqt):
    return jnp.exp2(dot(vp, vqt, NN) * EXP_SCALE)


def forward_kernel(cfg, *refs):
    qlen, qtok, plen, store, where, n_packs = cfg
    packs = refs[:n_packs]
    info_ref, mine_ref, other_ref = refs[n_packs : n_packs + 3]
    stats_ref, total_ref, sums_ref, expo_ref, vqt_ref = refs[n_packs + 3 :]
    lo = info_ref[0]
    first_half, second_half = both_queries(lo, mine_ref, other_ref, slice(0, qtok))
    vqt_ref[:, :qtok] = jnp.transpose(first_half.astype(f32)).astype(bf16)
    vqt_ref[:, qtok:] = jnp.transpose(second_half.astype(f32)).astype(bf16)
    tail = slice(mine_ref.shape[0] - 16, mine_ref.shape[0])
    rows = jnp.maximum(mine_ref[tail, :].astype(f32), other_ref[tail, :].astype(f32))

    def forward(pack, p, pos):
        expo = expo_of(pack[p, :plen, :], vqt_ref[...])
        total_ref[pl.ds(pos, 1), :] = jnp.sum(expo, axis=0, keepdims=True)
        if store:
            expo_ref[pos] = expo.astype(bf16)
        hi, core = where(info_ref, pos)
        here = (rows == ((hi * 2 + lo) * 2 + core).astype(f32)).astype(f32)
        stats_ref[1, pl.ds(pos, 1), :] = jnp.sum(here, axis=0, keepdims=True)
        stats_ref[2, pl.ds(pos, 1), :] = here[:1, :]

    over_packs(packs, forward)
    same = same_query((2 * qtok, LANES), 0, qlen)
    logits = sum(dot(part, same, NN) for part in parts_of(jnp.log(total_ref[...]), 3)) * (1.0 / qlen)
    stats_ref[0] = logits
    sums_ref[...] = jnp.zeros_like(sums_ref)
    sums_ref[:1, :] = jnp.sum(stats_ref[1] * jnp.exp(logits), axis=0, keepdims=True)
    sums_ref[1:2, :] = jnp.sum(stats_ref[2] * logits, axis=0, keepdims=True)


def backward_kernel(cfg, *refs):
    qlen, qtok, plen, store, where, n_packs = cfg
    packs = refs[:n_packs]
    info_ref, mine_ref, other_ref, up_ref, stats_ref, total_ref, sums_ref, recv_ref, expo_ref, vqt_ref = refs[
        n_packs : n_packs + 10
    ]
    refs = refs[n_packs + 10 :]
    n_parts = n_packs // 2 if store else 1
    part_refs, (dmine_ref, dother_ref, gup_ref, loss_ref) = refs[:n_parts], refs[n_parts : n_parts + 4]
    scale_ref, dvqt_ref, grad_ref, dv_ref, dvb_ref = refs[n_parts + 4 :]
    up = up_ref[...]
    rank = up.shape[0]
    lo = info_ref[0]
    vq = jnp.concatenate(both_queries(lo, mine_ref, other_ref, slice(0, qtok)), axis=0)
    logits, mult, first = stats_ref[0], stats_ref[1], stats_ref[2]
    summed = sums_ref[:1, :] + recv_ref[:1, :]
    live = lax.broadcasted_iota(jnp.int32, summed.shape, 1) < 2 * qtok // qlen
    summed = jnp.where(live, summed, 1.0)
    loss_ref[...] = jnp.broadcast_to(jnp.log(summed) - (sums_ref[1:2, :] + recv_ref[1:2, :]), loss_ref.shape)
    dscore = (mult * jnp.exp(logits) / summed - first) * (1.0 / loss_temp)
    same = same_query((LANES, 2 * qtok), 1, qlen)
    scale_ref[...] = sum(dot(part, same, NN) for part in parts_of(dscore, 2)) / (total_ref[...] * qlen)

    def scaled_low(pack, p):
        blocks = range(plen, plen + plen // LANES * rank, rank)
        return jnp.concatenate([pack[p, at : at + rank, :] for at in blocks], axis=1)

    def project_out(vp, dv):
        vpf = vp.astype(f32)
        return (dv - vpf * jnp.sum(vpf * dv, axis=1, keepdims=True)).astype(bf16)

    if store:
        for pos in range(n_packs):
            rows = slice(pos * plen, (pos + 1) * plen)
            grad_ref[rows, :] = (expo_ref[pos].astype(f32) * scale_ref[pos : pos + 1, :]).astype(bf16)
            dv_ref[rows, :] = dot(grad_ref[rows, :], vq, NN)
            dvqt = dot(packs[pos][0, :plen, :], grad_ref[rows, :], TN)
            dvqt_ref[...] = dvqt if pos == 0 else dvqt_ref[...] + dvqt
        for pos, pack in enumerate(packs):
            rows = slice(pos * plen, (pos + 1) * plen)
            dv = project_out(pack[0, :plen, :], dv_ref[rows, :])
            dvb_ref[rows, :] = dv
            part_refs[pos % n_parts][where(info_ref, pos)[1]] = dot(up, dv, NT).astype(bf16)
        lows = jnp.concatenate([scaled_low(pack, 0) for pack in packs], axis=1)
        gup = dot(lows, dvb_ref[...], NN)
    else:
        dvqt_ref[...] = jnp.zeros_like(dvqt_ref)
        gup_ref[...] = jnp.zeros_like(gup_ref)

        def backward(pack, p, pos):
            vp = pack[p, :plen, :]
            grad = (expo_of(vp, vqt_ref[...]) * scale_ref[pl.ds(pos, 1), :]).astype(bf16)
            dvqt_ref[...] += dot(vp, grad, TN)
            dv = project_out(vp, dot(grad, vq, NN))
            hi, core = where(info_ref, pos)
            part_refs[0][hi, core] = dot(up, dv, NT).astype(bf16)
            gup_ref[...] += dot(scaled_low(pack, p), dv, NN)

        over_packs(packs, backward)
        gup = gup_ref[...]

    vqt = vqt_ref[...].astype(f32)
    dvqt = dvqt_ref[...]
    dvqt = (dvqt - vqt * jnp.sum(vqt * dvqt, axis=0, keepdims=True)).astype(bf16)
    dlow = dot(up, dvqt, NN)
    dmine_ref[...] = jnp.where(lo == 0, dlow[:, :qtok], dlow[:, qtok:])
    dother_ref[...] = jnp.where(lo == 0, dlow[:, qtok:], dlow[:, :qtok]).astype(bf16)
    lows = [
        both_queries(lo, mine_ref, other_ref, slice(at, at + rank))
        for at in range(qtok, qtok + qtok // LANES * rank, rank)
    ]
    lows = jnp.concatenate([low[0] for low in lows] + [low[1] for low in lows], axis=1)
    gup_ref[...] = gup + dot(lows, dvqt, NT)


def places(steps):
    def where(info_ref, pos):
        n = len(steps)
        if n <= 8:
            return jnp.bitwise_xor(info_ref[1], steps[pos % n]), info_ref[2] if pos < n else 1 - info_ref[2]
        return lax.rem(pos, n), jnp.where(pos < n, info_ref[2], 1 - info_ref[2])

    return where


def score_forward(packs, steps, info, mine, other, qlen, qtok, plen):
    npos = 2 * len(steps)
    store = len(packs) == npos
    cfg = (qlen, qtok, plen, store, places(steps), len(packs))
    return pl.pallas_call(
        functools.partial(forward_kernel, cfg),
        in_specs=[VMEM] * len(packs) + [SMEM] + [VMEM] * 2,
        out_specs=[VMEM] * 5,
        out_shape=(
            jax.ShapeDtypeStruct((3, npos, LANES), f32),
            jax.ShapeDtypeStruct((npos, 2 * qtok), f32),
            jax.ShapeDtypeStruct((8, LANES), f32),
            jax.ShapeDtypeStruct((npos, plen, 2 * qtok) if store else (1, 16, LANES), bf16),
            jax.ShapeDtypeStruct((LANES, 2 * qtok), bf16),
        ),
        compiler_params=pltpu.CompilerParams(vmem_limit_bytes=(16 if store else 40) * 2**20),
        cost_estimate=cost(1.9),
        name="score_forward",
    )(*packs, info, mine, other)


def score_backward(packs, steps, info, mine, other, up, stats, total, sums, recv, expo, vqt, qlen, qtok, plen):
    npos, rank = 2 * len(steps), up.shape[0]
    store = len(packs) == npos
    cfg = (qlen, qtok, plen, store, places(steps), len(packs))
    part = jax.ShapeDtypeStruct((2, rank, plen), bf16)
    whole = jax.ShapeDtypeStruct((len(steps), 2, rank, plen), bf16)
    kept = npos * plen if store else 16
    parts = (part,) * len(steps) if store else (whole,)
    return pl.pallas_call(
        functools.partial(backward_kernel, cfg),
        in_specs=[VMEM] * len(packs) + [SMEM] + [VMEM] * 9,
        out_specs=[VMEM] * (len(parts) + 4),
        out_shape=(
            *parts,
            jax.ShapeDtypeStruct((rank, qtok), f32),
            jax.ShapeDtypeStruct((rank, qtok), bf16),
            jax.ShapeDtypeStruct((rank, LANES), f32),
            jax.ShapeDtypeStruct((8, LANES), f32),
        ),
        scratch_shapes=[
            pltpu.VMEM((npos, 2 * qtok), f32),
            pltpu.VMEM((LANES, 2 * qtok), f32),
            pltpu.VMEM((kept, 2 * qtok), bf16),
            pltpu.VMEM((kept, LANES), f32),
            pltpu.VMEM((kept, LANES), bf16),
        ],
        compiler_params=pltpu.CompilerParams(vmem_limit_bytes=(20 if store else 40) * 2**20),
        cost_estimate=cost(2.5),
        name="score_backward",
    )(*packs, info, mine, other, up, stats, total, sums, recv, expo, vqt)


def collect_kernel(n, *refs):
    parts, (mine_ref, recv_ref, r_ref, up_ref, out_ref) = refs[:n], refs[n:]
    _, _, plen = parts[0].shape
    qtok = mine_ref.shape[1]
    for i in range(2):
        out_ref[:, i * plen : (i + 1) * plen] = sum(part[i].astype(f32) for part in parts)
    out_ref[:, 2 * plen : 2 * plen + qtok] = (mine_ref[...] + recv_ref[...].astype(f32)) * r_ref[:1, :]
    out_ref[:, 2 * plen + qtok :] = up_ref[...]


def collect(parts, mine, recv, r, up):
    rank, qtok = mine.shape
    plen = parts[0].shape[2]
    return pl.pallas_call(
        functools.partial(collect_kernel, len(parts)),
        in_specs=[VMEM] * (len(parts) + 4),
        out_specs=VMEM,
        out_shape=jax.ShapeDtypeStruct((rank, 2 * plen + qtok + LANES), f32),
        compiler_params=pltpu.CompilerParams(vmem_limit_bytes=4 * 2**20),
        cost_estimate=cost(0.3),
        name="collect",
    )(*parts, mine, recv, r, up)


def grad_kernel(plen, qtok, info_ref, p_ref, q_ref, mine_ref, other_ref, r_mine_ref, r_other_ref, out_ref):
    core = info_ref[2]
    width = p_ref.shape[1]
    queries = slice(2 * plen, 2 * plen + qtok)
    q_mine, q_other = mine_ref[:, queries].astype(bf16), other_ref[:, queries].astype(bf16)
    q_dlow = [jnp.where(core == i, q_mine, q_other) for i in range(2)]
    p_dlow = []
    for i in range(2):
        r = jnp.where(core == i, r_mine_ref[:1, :plen], r_other_ref[:1, :plen])
        rows = slice(i * plen, (i + 1) * plen)
        p_dlow.append(((mine_ref[:, rows] + other_ref[:, rows]) * r).astype(bf16))
    total = dot(jnp.concatenate(q_dlow, axis=1), q_ref[...], NN)
    total += dot(jnp.concatenate(p_dlow, axis=1), p_ref[...], NN)
    out_ref[:, :width] = total.astype(bf16)
    out_ref[:, width:] = (mine_ref[:, 2 * plen + qtok :] + other_ref[:, 2 * plen + qtok :]).astype(bf16)


def grad_all(info, passage_rows, query_rows, mine, other, r_mine, r_other, plen, qtok):
    rank, width = mine.shape[0], passage_rows.shape[1]
    return pl.pallas_call(
        functools.partial(grad_kernel, plen, qtok),
        in_specs=[SMEM] + [VMEM] * 6,
        out_specs=VMEM,
        out_shape=jax.ShapeDtypeStruct((rank, width + LANES), bf16),
        compiler_params=pltpu.CompilerParams(vmem_limit_bytes=4 * 2**20),
        cost_estimate=cost(1.3),
        name="grad_all",
    )(info, passage_rows, query_rows, mine, other, r_mine, r_other)


def add_kernel(a_ref, b_ref, c_ref, d_ref, down_ref, up_ref):
    total = (a_ref[...].astype(f32) + d_ref[...].astype(f32)) + (
        b_ref[...].astype(f32) + c_ref[...].astype(f32)
    )
    width = down_ref.shape[1]
    down_ref[...] = total[:, :width]
    up_ref[...] = total[:, width:]


def add_four(parts, width):
    rank = parts[0].shape[0]
    return pl.pallas_call(
        add_kernel,
        in_specs=[VMEM] * 4,
        out_specs=[VMEM] * 2,
        out_shape=(
            jax.ShapeDtypeStruct((rank, width), f32),
            jax.ShapeDtypeStruct((rank, LANES), f32),
        ),
        compiler_params=pltpu.CompilerParams(vmem_limit_bytes=4 * 2**20),
        cost_estimate=cost(0.7),
        name="add_four",
    )(*parts)


def swap(x):
    return lax.ppermute(x, "sub", [(0, 1), (1, 0)])


def across(x, nshard, step):
    return lax.ppermute(x, "shard", [(i, i ^ step) for i in range(nshard)])


def gather_packs(pack, nshard, groups):
    if nshard == 8:
        pack = pack[None]
        near = [pack] + [across(pack, nshard, k) for k in (6, 4, 2)]
        return near + [swap(piece) for piece in near], (0, 3, 2, 1)
    near = lax.all_gather(pack, "shard", axis_index_groups=groups)
    return [near, swap(near)], tuple(range(nshard // 2))


def exchange_parts(parts, steps, nshard, groups):
    if len(parts) == 1:
        parts = lax.all_to_all(parts[0], "shard", split_axis=0, concat_axis=0, tiled=True, axis_index_groups=groups)
        return [jnp.sum(parts.astype(f32), axis=0)]
    return [parts[0]] + [across(part, nshard, 2 * step) for part, step in zip(parts[1:], steps[1:], strict=True)]


def sum_over_shards(x, nshard, width):
    if nshard != 8:
        x = lax.psum(x.astype(f32), "shard")
        return x[:, :width], x[:, width:]
    x = (x.astype(f32) + across(x, nshard, 1).astype(f32)).astype(bf16)
    return add_four([x] + [across(x, nshard, k) for k in (6, 4, 2)], width)


def per_device(
    query_hidden_states,
    passage_hidden_states,
    projection_matrix,
    adapter_down_weight,
    adapter_up_weight,
    passage_pair_index,
    passage_row_table,
):
    nshard = lax.axis_size("shard")
    core = lax.axis_index("sub").astype(jnp.int32)
    shard = lax.axis_index("shard").astype(jnp.int32)
    info = jnp.stack([shard % 2, shard // 2, core])
    groups = [list(range(parity, nshard, 2)) for parity in range(2)]
    qdev, qlen, width = query_hidden_states.shape
    pdev, plen, _ = passage_hidden_states.shape
    half = qdev // 2
    qtok = half * qlen
    query_rows = query_hidden_states.reshape(qdev * qlen, width)
    passage_rows = passage_hidden_states.reshape(pdev * plen, width)

    send_p, keep_p, query_vmem, weight = project_passages(
        info, passage_rows, query_rows, projection_matrix, jnp.transpose(adapter_down_weight)
    )
    send_q, keep_q = project_queries(info, query_vmem, weight, adapter_up_weight.shape[0])
    ppack, r_p = pack_passage(keep_p, swap(send_p), adapter_up_weight)
    mine, r_q = pack_queries(
        info, passage_row_table, jnp.transpose(passage_pair_index), keep_q, swap(send_q), adapter_up_weight
    )
    other = across(mine, nshard, 1)
    packs, steps = gather_packs(ppack, nshard, groups)
    mine, r_other = lax.optimization_barrier((mine, swap(r_p)))

    stats, total, sums, expo, vqt = score_forward(packs, steps, info, mine, other, qlen, qtok, plen)
    *parts, dlow_mine, dlow_other, gup, loss = score_backward(
        packs,
        steps,
        info,
        mine,
        other,
        adapter_up_weight,
        stats,
        total,
        sums,
        across(sums, nshard, 1),
        expo,
        vqt,
        qlen,
        qtok,
        plen,
    )
    parts = exchange_parts(parts, steps, nshard, groups)
    collected = collect(parts, dlow_mine, across(dlow_other, nshard, 1), r_q, gup)
    grads = grad_all(info, passage_rows, query_rows, collected, swap(collected), r_p, r_other, plen, qtok)
    query_loss = lax.dynamic_slice_in_dim(loss[0], info[0] * half, half, 0)
    down_sum, up_sum = sum_over_shards(grads, nshard, width)
    return (query_loss, jnp.transpose(down_sum), up_sum)


def solution(mesh):
    placed = (
        P(("groups", "shard"), None, "sub"),
        P(("groups", "shard"), None, "sub"),
        P("sub", None),
        P("sub", None),
        P(),
        P(("groups", "shard"), None),
        P("groups"),
    )
    return jax.shard_map(
        per_device,
        mesh=mesh,
        in_specs=placed,
        out_specs=(P(("groups", "shard", "sub")), P(("groups", "sub"), None), P("groups", None)),
        check_vma=False,
    )
```

```python
import functools
import math

import jax
import jax.numpy as jnp
from jax import lax
from jax.experimental import pallas as pl
from jax.experimental.pallas import tpu as pltpu
from jax.sharding import PartitionSpec as P

pool_temp = 0.05
loss_temp = 0.05
norm_eps = 1e-06
bf16 = jnp.bfloat16
f32 = jnp.float32
LANES = 128
EXP_SCALE = math.log2(math.e) / pool_temp
VMEM = pl.BlockSpec(memory_space=pltpu.VMEM)
SMEM = pl.BlockSpec(memory_space=pltpu.SMEM)
HBM = pl.BlockSpec(memory_space=pltpu.HBM)


def cost(microseconds):
    return pl.CostEstimate(
        flops=int(microseconds * 1.1e9), bytes_accessed=int(microseconds * 3.5e6), transcendentals=0
    )


def dot(a, b, contract, precision=None):
    return lax.dot_general(
        a, b, ((contract[0], contract[1]), ((), ())), precision=precision, preferred_element_type=f32
    )


NN = ((1,), (0,))
NT = ((1,), (1,))
TN = ((0,), (0,))


def put_projection(send_ref, keep_ref, projected, rank):
    tokens = projected.shape[0] // 2
    low = jnp.transpose(projected[:, LANES:])[:rank, :]
    for i, ref in enumerate((send_ref, keep_ref)):
        ref[:tokens, :] = projected[i * tokens : (i + 1) * tokens, :LANES]
        for t in range(tokens // LANES):
            at = i * tokens + t * LANES
            ref[tokens + t * rank : tokens + (t + 1) * rank, :] = low[:, at : at + LANES]


def project_passages_kernel(
    info_ref, p_hbm, q_hbm, proj_hbm, down_hbm, send_ref, keep_ref, q_ref, weight_ref, p_ref, down_ref, sems
):
    core = info_ref[2]
    weights = [
        pltpu.make_async_copy(down_hbm, down_ref, sems.at[0]),
        pltpu.make_async_copy(proj_hbm, weight_ref.at[:, :LANES], sems.at[1]),
    ]
    loads = []
    for source, to in ((p_hbm, p_ref), (q_hbm, q_ref)):
        half = source.shape[0] // 2
        for i, owner in enumerate((1 - core, core)):
            rows = pl.ds(pl.multiple_of(owner * half, LANES), half)
            copy = pltpu.make_async_copy(
                source.at[rows, :], to.at[i * half : (i + 1) * half, :], sems.at[2 + len(loads)]
            )
            loads.append(copy)
    for copy in weights + loads[:2]:
        copy.start()
    weights[0].wait()
    rank, width = down_ref.shape
    low = jnp.concatenate([down_ref[...].astype(f32), jnp.zeros((LANES - rank, width), f32)], axis=0)
    weight_ref[:, LANES:] = jnp.transpose(low).astype(bf16)
    weights[1].wait()
    for copy in loads[2:]:
        copy.start()
    for copy in loads[:2]:
        copy.wait()
    put_projection(send_ref, keep_ref, dot(p_ref[...], weight_ref[...], NN), rank)
    for copy in loads[2:]:
        copy.wait()


def project_passages(info, passage_rows, query_rows, projection, down):
    half, width = passage_rows.shape[0] // 2, passage_rows.shape[1]
    rank = down.shape[0]
    shape = jax.ShapeDtypeStruct((half + half // LANES * rank, LANES), f32)
    operands = (passage_rows, query_rows, projection, down)
    operands = [pltpu.with_memory_space_constraint(x, pltpu.HBM) for x in operands]
    return pl.pallas_call(
        project_passages_kernel,
        in_specs=[SMEM] + [HBM] * 4,
        out_specs=[VMEM] * 4,
        out_shape=(
            shape,
            shape,
            pltpu.VMEM(query_rows.shape, bf16),
            pltpu.VMEM((width, 2 * LANES), bf16),
        ),
        scratch_shapes=[
            pltpu.VMEM((2 * half, width), bf16),
            pltpu.VMEM((rank, width), bf16),
            pltpu.SemaphoreType.DMA((6,)),
        ],
        compiler_params=pltpu.CompilerParams(vmem_limit_bytes=8 * 2**20),
        cost_estimate=cost(3.7),
        name="project_passages",
    )(info, *operands)


def project_queries_kernel(rank, q_ref, weight_ref, send_ref, keep_ref):
    put_projection(send_ref, keep_ref, dot(q_ref[...], weight_ref[...], NN), rank)


def project_queries(query_rows, weight, rank):
    half = query_rows.shape[0] // 2
    shape = jax.ShapeDtypeStruct((half + half // LANES * rank, LANES), f32)
    return pl.pallas_call(
        functools.partial(project_queries_kernel, rank),
        in_specs=[VMEM] * 2,
        out_specs=[VMEM] * 2,
        out_shape=(shape, shape),
        compiler_params=pltpu.CompilerParams(vmem_limit_bytes=4 * 2**20),
        cost_estimate=cost(1.5),
        name="project_queries",
    )(query_rows, weight)


def pad_lanes(x):
    return jnp.concatenate([x, jnp.zeros((x.shape[0], LANES - x.shape[1]), x.dtype)], axis=1)


def pack_rows(keep_ref, recv_ref, up, out_ref, r_ref):
    rank, tokens = up.shape[0], r_ref.shape[1]
    for t in range(tokens // LANES):
        block = slice(t * LANES, (t + 1) * LANES)
        rows = slice(tokens + t * rank, tokens + (t + 1) * rank)
        low = (keep_ref[rows, :] + recv_ref[rows, :]).astype(bf16)
        full = keep_ref[block, :] + recv_ref[block, :] + dot(low, up, TN)
        r = lax.rsqrt(jnp.sum(full * full, axis=1, keepdims=True) + norm_eps)
        out_ref[block, :] = (full * r).astype(bf16)
        r = jnp.transpose(jnp.broadcast_to(r, (LANES, LANES)))
        out_ref[rows, :] = (low.astype(f32) * r[:rank, :]).astype(bf16)
        r_ref[:, block] = r[:8, :]


def pack_passage_kernel(keep_ref, recv_ref, up_ref, out_ref, r_ref):
    pack_rows(keep_ref, recv_ref, up_ref[...], out_ref, r_ref)


def pack_passage(keep, recv, up):
    rank = up.shape[0]
    tokens = keep.shape[0] // (LANES + rank) * LANES
    return pl.pallas_call(
        pack_passage_kernel,
        in_specs=[VMEM] * 3,
        out_specs=[VMEM] * 2,
        out_shape=(
            jax.ShapeDtypeStruct((tokens + tokens // LANES * rank, LANES), bf16),
            jax.ShapeDtypeStruct((8, tokens), f32),
        ),
        compiler_params=pltpu.CompilerParams(vmem_limit_bytes=4 * 2**20),
        cost_estimate=cost(6),
        name="pack_passage",
    )(keep, recv, up)


def pack_queries_kernel(info_ref, table_ref, ids_ref, keep_ref, recv_ref, up_ref, out_ref, r_ref):
    pack_rows(keep_ref, recv_ref, up_ref[...], out_ref, r_ref)
    ids = ids_ref[...]
    cands, qdev = ids.shape
    n_ids = table_ref.shape[0]
    if n_ids <= 16:
        rows = jnp.zeros(ids.shape, jnp.int32)
        for i in range(n_ids):
            rows = jnp.where(ids == i, table_ref[i], rows)
    else:
        rows = lax.fori_loop(
            0, n_ids, lambda i, c: jnp.where(ids == i, table_ref[i], c), jnp.zeros(ids.shape, jnp.int32)
        )
    half = qdev // 2
    wide = jnp.concatenate([pad_lanes(rows.astype(f32)), jnp.full((16 - cands, LANES), -1.0, f32)], axis=0)
    place = info_ref[0] * half
    wide = pltpu.roll(wide, lax.rem(place - info_ref[2] * half + LANES, LANES), 1)
    lane = lax.broadcasted_iota(jnp.int32, wide.shape, 1)
    wide = jnp.where((lane >= place) & (lane < place + half), wide, -1.0)
    out_ref[out_ref.shape[0] - 16 :, :] = wide.astype(bf16)


def pack_queries(info, table, ids, keep, recv, up):
    rank = up.shape[0]
    tokens = keep.shape[0] // (LANES + rank) * LANES
    return pl.pallas_call(
        pack_queries_kernel,
        in_specs=[SMEM] * 2 + [VMEM] * 4,
        out_specs=[VMEM] * 2,
        out_shape=(
            jax.ShapeDtypeStruct((tokens + tokens // LANES * rank + 16, LANES), bf16),
            jax.ShapeDtypeStruct((8, tokens), f32),
        ),
        compiler_params=pltpu.CompilerParams(vmem_limit_bytes=4 * 2**20),
        cost_estimate=cost(0.9),
        name="pack_queries",
    )(info, table, ids, keep, recv, up)


def both_queries(lo, mine_ref, other_ref, at):
    mine, other = mine_ref[at, :], other_ref[at, :]
    return jnp.where(lo == 0, mine, other), jnp.where(lo == 0, other, mine)


def over_packs(packs, body):
    at = 0
    for pack in packs:
        n = pack.shape[0]
        if n <= 8:
            for p in range(n):
                body(pack, p, at + p)
        else:
            lax.fori_loop(0, n, lambda p, c, pack=pack, at=at: (body(pack, p, at + p), c)[1], 0)
        at += n


def same_query(shape, dim, qlen):
    token = lax.broadcasted_iota(jnp.int32, shape, dim) // qlen
    return (token == lax.broadcasted_iota(jnp.int32, shape, 1 - dim)).astype(bf16)


def parts_of(wide, n):
    parts = []
    for _ in range(n):
        parts.append(wide.astype(bf16))
        wide = wide - parts[-1].astype(f32)
    return parts


def expo_of(vp, vqt):
    return jnp.exp2(dot(vp, vqt, NN) * EXP_SCALE)


def forward_kernel(cfg, *refs):
    qlen, qtok, plen, store, where, n_packs = cfg
    packs = refs[:n_packs]
    info_ref, mine_ref, other_ref = refs[n_packs : n_packs + 3]
    stats_ref, total_ref, sums_ref, expo_ref, vqt_ref = refs[n_packs + 3 :]
    lo = info_ref[0]
    first_half, second_half = both_queries(lo, mine_ref, other_ref, slice(0, qtok))
    vqt_ref[:, :qtok] = jnp.transpose(first_half.astype(f32)).astype(bf16)
    vqt_ref[:, qtok:] = jnp.transpose(second_half.astype(f32)).astype(bf16)
    tail = slice(mine_ref.shape[0] - 16, mine_ref.shape[0])
    rows = jnp.maximum(mine_ref[tail, :].astype(f32), other_ref[tail, :].astype(f32))

    def forward(pack, p, pos):
        expo = expo_of(pack[p, :plen, :], vqt_ref[...])
        total_ref[pl.ds(pos, 1), :] = jnp.sum(expo, axis=0, keepdims=True)
        if store:
            expo_ref[pos] = expo.astype(bf16)
        hi, core = where(info_ref, pos)
        here = (rows == ((hi * 2 + lo) * 2 + core).astype(f32)).astype(f32)
        stats_ref[1, pl.ds(pos, 1), :] = jnp.sum(here, axis=0, keepdims=True)
        stats_ref[2, pl.ds(pos, 1), :] = here[:1, :]

    over_packs(packs, forward)
    same = same_query((2 * qtok, LANES), 0, qlen)
    logits = sum(dot(part, same, NN) for part in parts_of(jnp.log(total_ref[...]), 3)) * (1.0 / qlen)
    stats_ref[0] = logits
    sums_ref[...] = jnp.zeros_like(sums_ref)
    sums_ref[:1, :] = jnp.sum(stats_ref[1] * jnp.exp(logits), axis=0, keepdims=True)
    sums_ref[1:2, :] = jnp.sum(stats_ref[2] * logits, axis=0, keepdims=True)


def backward_kernel(cfg, *refs):
    qlen, qtok, plen, store, where, n_packs = cfg
    packs = refs[:n_packs]
    info_ref, mine_ref, other_ref, up_ref, stats_ref, total_ref, sums_ref, recv_ref = refs[n_packs : n_packs + 8]
    expo_ref, unit_ref, vqt_ref = refs[n_packs + 8 : n_packs + 11]
    refs = refs[n_packs + 11 :]
    n_parts = n_packs // 2 if store else 1
    part_refs, (dmine_ref, dother_ref, gup_ref, loss_ref) = refs[:n_parts], refs[n_parts : n_parts + 4]
    scale_ref, dvqt_ref, grad_ref, dv_ref, dvb_ref = refs[n_parts + 4 :]
    up = up_ref[...]
    rank = up.shape[0]
    lo = info_ref[0]
    vq = jnp.concatenate(both_queries(lo, mine_ref, other_ref, slice(0, qtok)), axis=0)
    logits, mult, first = stats_ref[0], stats_ref[1], stats_ref[2]
    summed = sums_ref[:1, :] + recv_ref[:1, :]
    live = lax.broadcasted_iota(jnp.int32, summed.shape, 1) < 2 * qtok // qlen
    summed = jnp.where(live, summed, 1.0)
    loss_ref[...] = jnp.broadcast_to(jnp.log(summed) - (sums_ref[1:2, :] + recv_ref[1:2, :]), loss_ref.shape)
    dscore = (mult * jnp.exp(logits) / summed - first) * (1.0 / loss_temp)
    same = same_query((LANES, 2 * qtok), 1, qlen)
    scale_ref[...] = sum(dot(part, same, NN) for part in parts_of(dscore, 2)) / (total_ref[...] * qlen)

    def scaled_low(pack, p):
        blocks = range(plen, plen + plen // LANES * rank, rank)
        return jnp.concatenate([pack[p, at : at + rank, :] for at in blocks], axis=1)

    def project_out(vp, dv):
        vpf = vp.astype(f32)
        return (dv - vpf * jnp.sum(vpf * dv, axis=1, keepdims=True)).astype(bf16)

    if store:
        for pos in range(n_packs):
            rows = slice(pos * plen, (pos + 1) * plen)
            grad_ref[rows, :] = (expo_ref[pos].astype(f32) * scale_ref[pos : pos + 1, :]).astype(bf16)
            dv_ref[rows, :] = dot(grad_ref[rows, :], vq, NN)
            dvqt = unit_ref[pos] * scale_ref[pos : pos + 1, :]
            dvqt_ref[...] = dvqt if pos == 0 else dvqt_ref[...] + dvqt
        for pos, pack in enumerate(packs):
            rows = slice(pos * plen, (pos + 1) * plen)
            dv = project_out(pack[0, :plen, :], dv_ref[rows, :])
            dvb_ref[rows, :] = dv
            part_refs[pos % n_parts][where(info_ref, pos)[1]] = dot(up, dv, NT).astype(bf16)
        lows = jnp.concatenate([scaled_low(pack, 0) for pack in packs], axis=1)
        gup = dot(lows, dvb_ref[...], NN)
    else:
        dvqt_ref[...] = jnp.zeros_like(dvqt_ref)
        gup_ref[...] = jnp.zeros_like(gup_ref)

        def backward(pack, p, pos):
            vp = pack[p, :plen, :]
            grad = (expo_of(vp, vqt_ref[...]) * scale_ref[pl.ds(pos, 1), :]).astype(bf16)
            dvqt_ref[...] += dot(vp, grad, TN)
            dv = project_out(vp, dot(grad, vq, NN))
            hi, core = where(info_ref, pos)
            part_refs[0][hi, core] = dot(up, dv, NT).astype(bf16)
            gup_ref[...] += dot(scaled_low(pack, p), dv, NN)

        over_packs(packs, backward)
        gup = gup_ref[...]

    vqt = vqt_ref[...].astype(f32)
    dvqt = dvqt_ref[...]
    dvqt = (dvqt - vqt * jnp.sum(vqt * dvqt, axis=0, keepdims=True)).astype(bf16)
    dlow = dot(up, dvqt, NN)
    dmine_ref[...] = jnp.where(lo == 0, dlow[:, :qtok], dlow[:, qtok:])
    dother_ref[...] = jnp.where(lo == 0, dlow[:, qtok:], dlow[:, :qtok]).astype(bf16)
    lows = [
        both_queries(lo, mine_ref, other_ref, slice(at, at + rank))
        for at in range(qtok, qtok + qtok // LANES * rank, rank)
    ]
    lows = jnp.concatenate([low[0] for low in lows] + [low[1] for low in lows], axis=1)
    gup_ref[...] = gup + dot(lows, dvqt, NT)


def places(steps):
    def where(info_ref, pos):
        n = len(steps)
        if n <= 8:
            return jnp.bitwise_xor(info_ref[1], steps[pos % n]), info_ref[2] if pos < n else 1 - info_ref[2]
        return lax.rem(pos, n), jnp.where(pos < n, info_ref[2], 1 - info_ref[2])

    return where


def score_forward(packs, steps, info, mine, other, qlen, qtok, plen):
    npos = 2 * len(steps)
    store = len(packs) == npos
    cfg = (qlen, qtok, plen, store, places(steps), len(packs))
    return pl.pallas_call(
        functools.partial(forward_kernel, cfg),
        in_specs=[VMEM] * len(packs) + [SMEM] + [VMEM] * 2,
        out_specs=[VMEM] * 5,
        out_shape=(
            jax.ShapeDtypeStruct((3, npos, LANES), f32),
            jax.ShapeDtypeStruct((npos, 2 * qtok), f32),
            jax.ShapeDtypeStruct((8, LANES), f32),
            jax.ShapeDtypeStruct((npos, plen, 2 * qtok) if store else (1, 16, LANES), bf16),
            jax.ShapeDtypeStruct((LANES, 2 * qtok), bf16),
        ),
        compiler_params=pltpu.CompilerParams(vmem_limit_bytes=(16 if store else 40) * 2**20),
        cost_estimate=cost(1.9),
        name="score_forward",
    )(*packs, info, mine, other)


def unit_kernel(plen, *refs):
    packs, (expo_ref, unit_ref) = refs[:-2], refs[-2:]
    for pos, pack in enumerate(packs):
        unit_ref[pos] = dot(pack[0, :plen, :], expo_ref[pos], TN)


def unit_of(packs, expo):
    npos, plen, ntok = expo.shape
    if npos != len(packs):
        return jnp.zeros((1, 8, LANES), f32)
    return pl.pallas_call(
        functools.partial(unit_kernel, plen),
        in_specs=[VMEM] * (npos + 1),
        out_specs=VMEM,
        out_shape=jax.ShapeDtypeStruct((npos, LANES, ntok), f32),
        compiler_params=pltpu.CompilerParams(vmem_limit_bytes=4 * 2**20),
        cost_estimate=cost(1.2),
        name="unit",
    )(*packs, expo)


def score_backward(packs, steps, info, mine, other, up, stats, total, sums, recv, expo, unit, vqt, qlen, qtok, plen):
    npos, rank = 2 * len(steps), up.shape[0]
    store = len(packs) == npos
    cfg = (qlen, qtok, plen, store, places(steps), len(packs))
    part = jax.ShapeDtypeStruct((2, rank, plen), bf16)
    whole = jax.ShapeDtypeStruct((len(steps), 2, rank, plen), bf16)
    kept = npos * plen if store else 16
    parts = (part,) * len(steps) if store else (whole,)
    return pl.pallas_call(
        functools.partial(backward_kernel, cfg),
        in_specs=[VMEM] * len(packs) + [SMEM] + [VMEM] * 10,
        out_specs=[VMEM] * (len(parts) + 4),
        out_shape=(
            *parts,
            jax.ShapeDtypeStruct((rank, qtok), f32),
            jax.ShapeDtypeStruct((rank, qtok), bf16),
            jax.ShapeDtypeStruct((rank, LANES), f32),
            jax.ShapeDtypeStruct((8, LANES), f32),
        ),
        scratch_shapes=[
            pltpu.VMEM((npos, 2 * qtok), f32),
            pltpu.VMEM((LANES, 2 * qtok), f32),
            pltpu.VMEM((kept, 2 * qtok), bf16),
            pltpu.VMEM((kept, LANES), f32),
            pltpu.VMEM((kept, LANES), bf16),
        ],
        compiler_params=pltpu.CompilerParams(vmem_limit_bytes=(20 if store else 40) * 2**20),
        cost_estimate=cost(2.5),
        name="score_backward",
    )(*packs, info, mine, other, up, stats, total, sums, recv, expo, unit, vqt)


def collect_kernel(n, *refs):
    parts, (mine_ref, recv_ref, r_ref, r_p_ref, up_ref, out_ref) = refs[:n], refs[n:]
    _, _, plen = parts[0].shape
    qtok = mine_ref.shape[1]
    for i in range(2):
        out_ref[:, i * plen : (i + 1) * plen] = sum(part[i].astype(f32) for part in parts)
    out_ref[:, 2 * plen : 2 * plen + qtok] = (mine_ref[...] + recv_ref[...].astype(f32)) * r_ref[:1, :]
    out_ref[:, 2 * plen + qtok : 2 * plen + qtok + LANES] = up_ref[...]
    out_ref[:, 2 * plen + qtok + LANES :] = jnp.broadcast_to(r_p_ref[:1, :], (out_ref.shape[0], plen))


def collect(parts, mine, recv, r, r_p, up):
    rank, qtok = mine.shape
    plen = parts[0].shape[2]
    return pl.pallas_call(
        functools.partial(collect_kernel, len(parts)),
        in_specs=[VMEM] * (len(parts) + 5),
        out_specs=VMEM,
        out_shape=jax.ShapeDtypeStruct((rank, 3 * plen + qtok + LANES), f32),
        compiler_params=pltpu.CompilerParams(vmem_limit_bytes=4 * 2**20),
        cost_estimate=cost(0.3),
        name="collect",
    )(*parts, mine, recv, r, r_p, up)


def grad_kernel(plen, qtok, info_ref, p_ref, q_ref, mine_ref, other_ref, out_ref):
    core = info_ref[2]
    width = p_ref.shape[1]
    queries = slice(2 * plen, 2 * plen + qtok)
    q_mine, q_other = mine_ref[:, queries].astype(bf16), other_ref[:, queries].astype(bf16)
    q_dlow = [jnp.where(core == i, q_mine, q_other) for i in range(2)]
    p_dlow = []
    for i in range(2):
        r = jnp.where(core == i, mine_ref[:, -plen:], other_ref[:, -plen:])
        rows = slice(i * plen, (i + 1) * plen)
        p_dlow.append(((mine_ref[:, rows] + other_ref[:, rows]) * r).astype(bf16))
    total = dot(jnp.concatenate(q_dlow, axis=1), q_ref[...], NN)
    total += dot(jnp.concatenate(p_dlow, axis=1), p_ref[...], NN)
    out_ref[:, :width] = total.astype(bf16)
    ups = slice(2 * plen + qtok, 2 * plen + qtok + LANES)
    out_ref[:, width:] = (mine_ref[:, ups] + other_ref[:, ups]).astype(bf16)


def grad_all(info, passage_rows, query_rows, mine, other, plen, qtok):
    rank, width = mine.shape[0], passage_rows.shape[1]
    return pl.pallas_call(
        functools.partial(grad_kernel, plen, qtok),
        in_specs=[SMEM] + [VMEM] * 4,
        out_specs=VMEM,
        out_shape=jax.ShapeDtypeStruct((rank, width + LANES), bf16),
        compiler_params=pltpu.CompilerParams(vmem_limit_bytes=4 * 2**20),
        cost_estimate=cost(1.3),
        name="grad_all",
    )(info, passage_rows, query_rows, mine, other)


def add_kernel(a_ref, b_ref, c_ref, d_ref, down_ref, up_ref):
    total = (a_ref[...].astype(f32) + b_ref[...].astype(f32)) + (
        c_ref[...].astype(f32) + d_ref[...].astype(f32)
    )
    width = down_ref.shape[1]
    down_ref[...] = total[:, :width]
    up_ref[...] = total[:, width:]


def add_four(parts, width):
    rank = parts[0].shape[0]
    return pl.pallas_call(
        add_kernel,
        in_specs=[VMEM] * 4,
        out_specs=[VMEM] * 2,
        out_shape=(
            jax.ShapeDtypeStruct((rank, width), f32),
            jax.ShapeDtypeStruct((rank, LANES), f32),
        ),
        compiler_params=pltpu.CompilerParams(vmem_limit_bytes=4 * 2**20),
        cost_estimate=cost(0.7),
        name="add_four",
    )(*parts)


def swap(x):
    return lax.ppermute(x, "sub", [(0, 1), (1, 0)])


def across(x, nshard, step):
    return lax.ppermute(x, "shard", [(i, i ^ step) for i in range(nshard)])


def gather_packs(pack, nshard, groups):
    if nshard == 8:
        pack = pack[None]
        near = [pack] + [across(pack, nshard, k) for k in (2, 4, 6)]
        return near + [swap(piece) for piece in near], (0, 1, 2, 3)
    near = lax.all_gather(pack, "shard", axis_index_groups=groups)
    return [near, swap(near)], tuple(range(nshard // 2))


def exchange_parts(parts, steps, nshard, groups):
    if len(parts) == 1:
        parts = lax.all_to_all(parts[0], "shard", split_axis=0, concat_axis=0, tiled=True, axis_index_groups=groups)
        return [jnp.sum(parts.astype(f32), axis=0)]
    return [parts[0]] + [across(part, nshard, 2 * step) for part, step in reversed([*zip(parts, steps, strict=True)][1:])]


def sum_over_shards(x, nshard, width):
    if nshard != 8:
        x = lax.psum(x.astype(f32), "shard")
        return x[:, :width], x[:, width:]
    x = (x.astype(f32) + across(x, nshard, 1).astype(f32)).astype(bf16)
    return add_four([x] + [across(x, nshard, k) for k in (2, 4, 6)], width)


def per_device(
    query_hidden_states,
    passage_hidden_states,
    projection_matrix,
    adapter_down_weight,
    adapter_up_weight,
    passage_pair_index,
    passage_row_table,
):
    nshard = lax.axis_size("shard")
    core = lax.axis_index("sub").astype(jnp.int32)
    shard = lax.axis_index("shard").astype(jnp.int32)
    info = jnp.stack([shard % 2, shard // 2, core])
    groups = [list(range(parity, nshard, 2)) for parity in range(2)]
    qdev, qlen, width = query_hidden_states.shape
    pdev, plen, _ = passage_hidden_states.shape
    half = qdev // 2
    qtok = half * qlen
    query_rows = query_hidden_states.reshape(qdev * qlen, width)
    passage_rows = passage_hidden_states.reshape(pdev * plen, width)

    send_p, keep_p, query_vmem, weight = project_passages(
        info, passage_rows, query_rows, projection_matrix, jnp.transpose(adapter_down_weight)
    )
    send_q, keep_q = project_queries(query_vmem, weight, adapter_up_weight.shape[0])
    ppack, r_p = pack_passage(keep_p, swap(send_p), adapter_up_weight)
    mine, r_q = pack_queries(
        info, passage_row_table, jnp.transpose(passage_pair_index), keep_q, swap(send_q), adapter_up_weight
    )
    other = across(mine, nshard, 1)
    packs, steps = gather_packs(ppack, nshard, groups)

    stats, total, sums, expo, vqt = score_forward(packs, steps, info, mine, other, qlen, qtok, plen)
    *parts, dlow_mine, dlow_other, gup, loss = score_backward(
        packs,
        steps,
        info,
        mine,
        other,
        adapter_up_weight,
        stats,
        total,
        sums,
        across(sums, nshard, 1),
        expo,
        unit_of(packs, expo),
        vqt,
        qlen,
        qtok,
        plen,
    )
    parts = exchange_parts(parts, steps, nshard, groups)
    collected = collect(parts, dlow_mine, across(dlow_other, nshard, 1), r_q, r_p, gup)
    grads = grad_all(info, passage_rows, query_rows, collected, swap(collected), plen, qtok)
    query_loss = lax.dynamic_slice_in_dim(loss[0], info[0] * half, half, 0)
    down_sum, up_sum = sum_over_shards(grads, nshard, width)
    return (query_loss, jnp.transpose(down_sum), up_sum)


def solution(mesh):
    placed = (
        P(("groups", "shard"), None, "sub"),
        P(("groups", "shard"), None, "sub"),
        P("sub", None),
        P("sub", None),
        P(),
        P(("groups", "shard"), None),
        P("groups"),
    )
    return jax.shard_map(
        per_device,
        mesh=mesh,
        in_specs=placed,
        out_specs=(P(("groups", "shard", "sub")), P(("groups", "sub"), None), P("groups", None)),
        check_vma=False,
    )
```

```python
import functools
import math

import jax
import jax.numpy as jnp
from jax import lax
from jax.experimental import pallas as pl
from jax.experimental.pallas import tpu as pltpu
from jax.sharding import PartitionSpec as P

pool_temp = 0.05
loss_temp = 0.05
norm_eps = 1e-06
bf16 = jnp.bfloat16
f32 = jnp.float32
LANES = 128
EXP_SCALE = math.log2(math.e) / pool_temp
VMEM = pl.BlockSpec(memory_space=pltpu.VMEM)
SMEM = pl.BlockSpec(memory_space=pltpu.SMEM)
HBM = pl.BlockSpec(memory_space=pltpu.HBM)


def cost(microseconds):
    return pl.CostEstimate(
        flops=int(microseconds * 1.1e9), bytes_accessed=int(microseconds * 3.5e6), transcendentals=0
    )


def dot(a, b, contract, precision=None):
    return lax.dot_general(
        a, b, ((contract[0], contract[1]), ((), ())), precision=precision, preferred_element_type=f32
    )


NN = ((1,), (0,))
NT = ((1,), (1,))
TN = ((0,), (0,))


def put_projection(send_ref, keep_ref, projected, rank):
    tokens = projected.shape[0] // 2
    low = jnp.transpose(projected[:, LANES:])[:rank, :]
    for i, ref in enumerate((send_ref, keep_ref)):
        ref[:tokens, :] = projected[i * tokens : (i + 1) * tokens, :LANES]
        for t in range(tokens // LANES):
            at = i * tokens + t * LANES
            ref[tokens + t * rank : tokens + (t + 1) * rank, :] = low[:, at : at + LANES]


def project_passages_kernel(
    info_ref, p_hbm, q_hbm, proj_hbm, down_hbm, send_ref, keep_ref, q_ref, weight_ref, p_ref, down_ref, sems
):
    core = info_ref[2]
    weights = [
        pltpu.make_async_copy(down_hbm, down_ref, sems.at[0]),
        pltpu.make_async_copy(proj_hbm, weight_ref.at[:, :LANES], sems.at[1]),
    ]
    loads = []
    for source, to in ((p_hbm, p_ref), (q_hbm, q_ref)):
        half = source.shape[0] // 2
        for i, owner in enumerate((1 - core, core)):
            rows = pl.ds(pl.multiple_of(owner * half, LANES), half)
            copy = pltpu.make_async_copy(
                source.at[rows, :], to.at[i * half : (i + 1) * half, :], sems.at[2 + len(loads)]
            )
            loads.append(copy)
    for copy in weights + loads[:2]:
        copy.start()
    weights[0].wait()
    rank, width = down_ref.shape
    low = jnp.concatenate([down_ref[...].astype(f32), jnp.zeros((LANES - rank, width), f32)], axis=0)
    weight_ref[:, LANES:] = jnp.transpose(low).astype(bf16)
    weights[1].wait()
    for copy in loads[2:]:
        copy.start()
    for copy in loads[:2]:
        copy.wait()
    put_projection(send_ref, keep_ref, dot(p_ref[...], weight_ref[...], NN), rank)
    for copy in loads[2:]:
        copy.wait()


def project_passages(info, passage_rows, query_rows, projection, down):
    half, width = passage_rows.shape[0] // 2, passage_rows.shape[1]
    rank = down.shape[0]
    shape = jax.ShapeDtypeStruct((half + half // LANES * rank, LANES), f32)
    operands = (passage_rows, query_rows, projection, down)
    operands = [pltpu.with_memory_space_constraint(x, pltpu.HBM) for x in operands]
    return pl.pallas_call(
        project_passages_kernel,
        in_specs=[SMEM] + [HBM] * 4,
        out_specs=[VMEM] * 4,
        out_shape=(
            shape,
            shape,
            pltpu.VMEM(query_rows.shape, bf16),
            pltpu.VMEM((width, 2 * LANES), bf16),
        ),
        scratch_shapes=[
            pltpu.VMEM((2 * half, width), bf16),
            pltpu.VMEM((rank, width), bf16),
            pltpu.SemaphoreType.DMA((6,)),
        ],
        compiler_params=pltpu.CompilerParams(vmem_limit_bytes=8 * 2**20),
        cost_estimate=cost(3.7),
        name="project_passages",
    )(info, *operands)


def project_queries_kernel(rank, q_ref, weight_ref, send_ref, keep_ref):
    put_projection(send_ref, keep_ref, dot(q_ref[...], weight_ref[...], NN), rank)


def project_queries(query_rows, weight, rank):
    half = query_rows.shape[0] // 2
    shape = jax.ShapeDtypeStruct((half + half // LANES * rank, LANES), f32)
    return pl.pallas_call(
        functools.partial(project_queries_kernel, rank),
        in_specs=[VMEM] * 2,
        out_specs=[VMEM] * 2,
        out_shape=(shape, shape),
        compiler_params=pltpu.CompilerParams(vmem_limit_bytes=4 * 2**20),
        cost_estimate=cost(1.5),
        name="project_queries",
    )(query_rows, weight)


def pad_lanes(x):
    return jnp.concatenate([x, jnp.zeros((x.shape[0], LANES - x.shape[1]), x.dtype)], axis=1)


def pack_rows(keep_ref, recv_ref, up, out_ref, r_ref):
    rank, tokens = up.shape[0], r_ref.shape[1]
    for t in range(tokens // LANES):
        block = slice(t * LANES, (t + 1) * LANES)
        rows = slice(tokens + t * rank, tokens + (t + 1) * rank)
        low = (keep_ref[rows, :] + recv_ref[rows, :]).astype(bf16)
        full = keep_ref[block, :] + recv_ref[block, :] + dot(low, up, TN)
        r = lax.rsqrt(jnp.sum(full * full, axis=1, keepdims=True) + norm_eps)
        out_ref[block, :] = (full * r).astype(bf16)
        r = jnp.transpose(jnp.broadcast_to(r, (LANES, LANES)))
        out_ref[rows, :] = (low.astype(f32) * r[:rank, :]).astype(bf16)
        r_ref[:, block] = r[:8, :]


def pack_passage_kernel(keep_ref, recv_ref, up_ref, out_ref, r_ref):
    pack_rows(keep_ref, recv_ref, up_ref[...], out_ref, r_ref)


def pack_passage(keep, recv, up):
    rank = up.shape[0]
    tokens = keep.shape[0] // (LANES + rank) * LANES
    return pl.pallas_call(
        pack_passage_kernel,
        in_specs=[VMEM] * 3,
        out_specs=[VMEM] * 2,
        out_shape=(
            jax.ShapeDtypeStruct((tokens + tokens // LANES * rank, LANES), bf16),
            jax.ShapeDtypeStruct((8, tokens), f32),
        ),
        compiler_params=pltpu.CompilerParams(vmem_limit_bytes=4 * 2**20),
        cost_estimate=cost(6),
        name="pack_passage",
    )(keep, recv, up)


def pack_queries_kernel(info_ref, table_ref, ids_ref, keep_ref, recv_ref, up_ref, out_ref, r_ref):
    pack_rows(keep_ref, recv_ref, up_ref[...], out_ref, r_ref)
    ids = ids_ref[...]
    cands, qdev = ids.shape
    n_ids = table_ref.shape[0]
    if n_ids <= 16:
        rows = jnp.zeros(ids.shape, jnp.int32)
        for i in range(n_ids):
            rows = jnp.where(ids == i, table_ref[i], rows)
    else:
        rows = lax.fori_loop(
            0, n_ids, lambda i, c: jnp.where(ids == i, table_ref[i], c), jnp.zeros(ids.shape, jnp.int32)
        )
    half = qdev // 2
    wide = jnp.concatenate([pad_lanes(rows.astype(f32)), jnp.full((16 - cands, LANES), -1.0, f32)], axis=0)
    place = info_ref[0] * half
    wide = pltpu.roll(wide, lax.rem(place - info_ref[2] * half + LANES, LANES), 1)
    lane = lax.broadcasted_iota(jnp.int32, wide.shape, 1)
    wide = jnp.where((lane >= place) & (lane < place + half), wide, -1.0)
    out_ref[out_ref.shape[0] - 16 :, :] = wide.astype(bf16)


def pack_queries(info, table, ids, keep, recv, up):
    rank = up.shape[0]
    tokens = keep.shape[0] // (LANES + rank) * LANES
    return pl.pallas_call(
        pack_queries_kernel,
        in_specs=[SMEM] * 2 + [VMEM] * 4,
        out_specs=[VMEM] * 2,
        out_shape=(
            jax.ShapeDtypeStruct((tokens + tokens // LANES * rank + 16, LANES), bf16),
            jax.ShapeDtypeStruct((8, tokens), f32),
        ),
        compiler_params=pltpu.CompilerParams(vmem_limit_bytes=4 * 2**20),
        cost_estimate=cost(0.9),
        name="pack_queries",
    )(info, table, ids, keep, recv, up)


def both_queries(lo, mine_ref, other_ref, at):
    mine, other = mine_ref[at, :], other_ref[at, :]
    return jnp.where(lo == 0, mine, other), jnp.where(lo == 0, other, mine)


def over_packs(packs, body):
    at = 0
    for pack in packs:
        n = pack.shape[0]
        if n <= 8:
            for p in range(n):
                body(pack, p, at + p)
        else:
            lax.fori_loop(0, n, lambda p, c, pack=pack, at=at: (body(pack, p, at + p), c)[1], 0)
        at += n


def same_query(shape, dim, qlen):
    token = lax.broadcasted_iota(jnp.int32, shape, dim) // qlen
    return (token == lax.broadcasted_iota(jnp.int32, shape, 1 - dim)).astype(bf16)


def parts_of(wide, n):
    parts = []
    for _ in range(n):
        parts.append(wide.astype(bf16))
        wide = wide - parts[-1].astype(f32)
    return parts


def expo_of(vp, vqt):
    return jnp.exp2(dot(vp, vqt, NN) * EXP_SCALE)


def forward_kernel(cfg, *refs):
    qlen, qtok, plen, store, where, n_packs = cfg
    packs = refs[:n_packs]
    info_ref, mine_ref, other_ref = refs[n_packs : n_packs + 3]
    stats_ref, total_ref, sums_ref, weights_ref, vqt_ref = refs[n_packs + 3 :]
    lo = info_ref[0]
    first_half, second_half = both_queries(lo, mine_ref, other_ref, slice(0, qtok))
    vqt_ref[:, :qtok] = jnp.transpose(first_half.astype(f32)).astype(bf16)
    vqt_ref[:, qtok:] = jnp.transpose(second_half.astype(f32)).astype(bf16)
    tail = slice(mine_ref.shape[0] - 16, mine_ref.shape[0])
    rows = jnp.maximum(mine_ref[tail, :].astype(f32), other_ref[tail, :].astype(f32))

    def forward(pack, p, pos):
        expo = expo_of(pack[p, :plen, :], vqt_ref[...])
        total = jnp.sum(expo, axis=0, keepdims=True)
        total_ref[pl.ds(pos, 1), :] = total
        if store:
            weights_ref[pos] = (expo * (1.0 / total)).astype(bf16)
        hi, core = where(info_ref, pos)
        here = (rows == ((hi * 2 + lo) * 2 + core).astype(f32)).astype(f32)
        stats_ref[1, pl.ds(pos, 1), :] = jnp.sum(here, axis=0, keepdims=True)
        stats_ref[2, pl.ds(pos, 1), :] = here[:1, :]

    over_packs(packs, forward)
    same = same_query((2 * qtok, LANES), 0, qlen)
    logits = sum(dot(part, same, NN) for part in parts_of(jnp.log(total_ref[...]), 3)) * (1.0 / qlen)
    stats_ref[0] = logits
    sums_ref[...] = jnp.zeros_like(sums_ref)
    sums_ref[:1, :] = jnp.sum(stats_ref[1] * jnp.exp(logits), axis=0, keepdims=True)
    sums_ref[1:2, :] = jnp.sum(stats_ref[2] * logits, axis=0, keepdims=True)


def backward_kernel(cfg, *refs):
    qlen, qtok, plen, store, where, n_packs = cfg
    packs = refs[:n_packs]
    info_ref, mine_ref, other_ref, up_ref, stats_ref, total_ref, sums_ref, recv_ref = refs[n_packs : n_packs + 8]
    weights_ref, unit_ref, vqt_ref = refs[n_packs + 8 : n_packs + 11]
    refs = refs[n_packs + 11 :]
    n_parts = n_packs // 2 if store else 1
    part_refs, (dmine_ref, dother_ref, gup_ref, loss_ref) = refs[:n_parts], refs[n_parts : n_parts + 4]
    scale_ref, dvqt_ref, grad_ref, dv_ref, dvb_ref = refs[n_parts + 4 :]
    up = up_ref[...]
    rank = up.shape[0]
    lo = info_ref[0]
    vq = jnp.concatenate(both_queries(lo, mine_ref, other_ref, slice(0, qtok)), axis=0)
    logits, mult, first = stats_ref[0], stats_ref[1], stats_ref[2]
    summed = sums_ref[:1, :] + recv_ref[:1, :]
    live = lax.broadcasted_iota(jnp.int32, summed.shape, 1) < 2 * qtok // qlen
    summed = jnp.where(live, summed, 1.0)
    loss_ref[...] = jnp.broadcast_to(jnp.log(summed) - (sums_ref[1:2, :] + recv_ref[1:2, :]), loss_ref.shape)
    dscore = (mult * jnp.exp(logits) / summed - first) * (1.0 / loss_temp)
    same = same_query((LANES, 2 * qtok), 1, qlen)
    scale_ref[...] = sum(dot(part, same, NN) for part in parts_of(dscore, 3))

    def scaled_low(pack, p):
        blocks = range(plen, plen + plen // LANES * rank, rank)
        return jnp.concatenate([pack[p, at : at + rank, :] for at in blocks], axis=1)

    def project_out(vp, dv):
        vpf = vp.astype(f32)
        return parts_of(dv - vpf * jnp.sum(vpf * dv, axis=1, keepdims=True), 2)

    if store:
        for pos in range(n_packs):
            rows = slice(pos * plen, (pos + 1) * plen)
            grad_ref[rows, :] = (weights_ref[pos].astype(f32) * (scale_ref[pos : pos + 1, :] * (1.0 / qlen))).astype(bf16)
            dv_ref[rows, :] = dot(grad_ref[rows, :], vq, NN)
            dvqt = unit_ref[pos].astype(f32) * scale_ref[pos : pos + 1, :]
            dvqt_ref[...] = dvqt if pos == 0 else dvqt_ref[...] + dvqt
        for pos, pack in enumerate(packs):
            rows = slice(pos * plen, (pos + 1) * plen)
            dv = project_out(pack[0, :plen, :], dv_ref[rows, :])
            dvb_ref[0, rows, :], dvb_ref[1, rows, :] = dv
            part_refs[pos % n_parts][where(info_ref, pos)[1]] = (dot(up, dv[0], NT) + dot(up, dv[1], NT))
        lows = jnp.concatenate([scaled_low(pack, 0) for pack in packs], axis=1)
        gup = dot(lows, dvb_ref[0], NN) + dot(lows, dvb_ref[1], NN)
    else:
        dvqt_ref[...] = jnp.zeros_like(dvqt_ref)
        gup_ref[...] = jnp.zeros_like(gup_ref)

        def backward(pack, p, pos):
            vp = pack[p, :plen, :]
            scale = scale_ref[pl.ds(pos, 1), :]
            weights = (expo_of(vp, vqt_ref[...]) * (1.0 / total_ref[pl.ds(pos, 1), :])).astype(bf16)
            unit = (dot(vp, weights, TN) * (1.0 / qlen)).astype(bf16)
            dvqt_ref[...] += unit.astype(f32) * scale
            grad = (weights.astype(f32) * (scale * (1.0 / qlen))).astype(bf16)
            dv = project_out(vp, dot(grad, vq, NN))
            hi, core = where(info_ref, pos)
            part_refs[0][hi, core] = (dot(up, dv[0], NT) + dot(up, dv[1], NT))
            low = scaled_low(pack, p)
            gup_ref[...] += dot(low, dv[0], NN) + dot(low, dv[1], NN)

        over_packs(packs, backward)
        gup = gup_ref[...]

    vqt = vqt_ref[...].astype(f32)
    dvqt = dvqt_ref[...]
    dvqt = parts_of(dvqt - vqt * jnp.sum(vqt * dvqt, axis=0, keepdims=True), 2)
    dlow = dot(up, dvqt[0], NN) + dot(up, dvqt[1], NN)
    dmine_ref[...] = jnp.where(lo == 0, dlow[:, :qtok], dlow[:, qtok:])
    dother_ref[...] = jnp.where(lo == 0, dlow[:, qtok:], dlow[:, :qtok])
    lows = [
        both_queries(lo, mine_ref, other_ref, slice(at, at + rank))
        for at in range(qtok, qtok + qtok // LANES * rank, rank)
    ]
    lows = jnp.concatenate([low[0] for low in lows] + [low[1] for low in lows], axis=1)
    gup_ref[...] = gup + dot(lows, dvqt[0], NT) + dot(lows, dvqt[1], NT)


def places(steps):
    def where(info_ref, pos):
        n = len(steps)
        if n == 4:
            return jnp.bitwise_xor(info_ref[1], steps[pos % n]), info_ref[2] if pos < n else 1 - info_ref[2]
        return lax.rem(pos, n), jnp.where(pos < n, info_ref[2], 1 - info_ref[2])

    return where


def score_forward(packs, steps, info, mine, other, qlen, qtok, plen):
    npos = 2 * len(steps)
    store = len(packs) == npos
    cfg = (qlen, qtok, plen, store, places(steps), len(packs))
    return pl.pallas_call(
        functools.partial(forward_kernel, cfg),
        in_specs=[VMEM] * len(packs) + [SMEM] + [VMEM] * 2,
        out_specs=[VMEM] * 5,
        out_shape=(
            jax.ShapeDtypeStruct((3, npos, LANES), f32),
            jax.ShapeDtypeStruct((npos, 2 * qtok), f32),
            jax.ShapeDtypeStruct((8, LANES), f32),
            jax.ShapeDtypeStruct((npos, plen, 2 * qtok) if store else (1, 16, LANES), bf16),
            jax.ShapeDtypeStruct((LANES, 2 * qtok), bf16),
        ),
        compiler_params=pltpu.CompilerParams(vmem_limit_bytes=(16 if store else 40) * 2**20),
        cost_estimate=cost(1.9),
        name="score_forward",
    )(*packs, info, mine, other)


def unit_kernel(qlen, plen, *refs):
    packs, (weights_ref, unit_ref) = refs[:-2], refs[-2:]
    for pos, pack in enumerate(packs):
        unit_ref[pos] = (dot(pack[0, :plen, :], weights_ref[pos], TN) * (1.0 / qlen)).astype(bf16)


def unit_of(packs, weights, qlen):
    npos, plen, ntok = weights.shape
    if npos != len(packs):
        return jnp.zeros((1, 16, LANES), bf16)
    return pl.pallas_call(
        functools.partial(unit_kernel, qlen, plen),
        in_specs=[VMEM] * (npos + 1),
        out_specs=VMEM,
        out_shape=jax.ShapeDtypeStruct((npos, LANES, ntok), bf16),
        compiler_params=pltpu.CompilerParams(vmem_limit_bytes=4 * 2**20),
        cost_estimate=cost(1.2),
        name="unit",
    )(*packs, weights)


def score_backward(packs, steps, info, mine, other, up, stats, total, sums, recv, weights, unit, vqt, qlen, qtok, plen):
    npos, rank = 2 * len(steps), up.shape[0]
    store = len(packs) == npos
    cfg = (qlen, qtok, plen, store, places(steps), len(packs))
    part = jax.ShapeDtypeStruct((2, rank, plen), f32)
    whole = jax.ShapeDtypeStruct((len(steps), 2, rank, plen), f32)
    kept = npos * plen if store else 16
    parts = (part,) * len(steps) if store else (whole,)
    return pl.pallas_call(
        functools.partial(backward_kernel, cfg),
        in_specs=[VMEM] * len(packs) + [SMEM] + [VMEM] * 10,
        out_specs=[VMEM] * (len(parts) + 4),
        out_shape=(
            *parts,
            jax.ShapeDtypeStruct((rank, qtok), f32),
            jax.ShapeDtypeStruct((rank, qtok), f32),
            jax.ShapeDtypeStruct((rank, LANES), f32),
            jax.ShapeDtypeStruct((8, LANES), f32),
        ),
        scratch_shapes=[
            pltpu.VMEM((npos, 2 * qtok), f32),
            pltpu.VMEM((LANES, 2 * qtok), f32),
            pltpu.VMEM((kept, 2 * qtok), bf16),
            pltpu.VMEM((kept, LANES), f32),
            pltpu.VMEM((2, kept, LANES), bf16),
        ],
        compiler_params=pltpu.CompilerParams(vmem_limit_bytes=(20 if store else 40) * 2**20),
        cost_estimate=cost(2.5),
        name="score_backward",
    )(*packs, info, mine, other, up, stats, total, sums, recv, weights, unit, vqt)


def collect_kernel(n, *refs):
    parts, (mine_ref, recv_ref, r_ref, r_p_ref, up_ref, out_ref) = refs[:n], refs[n:]
    _, _, plen = parts[0].shape
    qtok = mine_ref.shape[1]
    for i in range(2):
        out_ref[:, i * plen : (i + 1) * plen] = sum(part[i].astype(f32) for part in parts)
    out_ref[:, 2 * plen : 2 * plen + qtok] = (mine_ref[...] + recv_ref[...].astype(f32)) * r_ref[:1, :]
    out_ref[:, 2 * plen + qtok : 2 * plen + qtok + LANES] = up_ref[...]
    out_ref[:, 2 * plen + qtok + LANES :] = jnp.broadcast_to(r_p_ref[:1, :], (out_ref.shape[0], plen))


def collect(parts, mine, recv, r, r_p, up):
    rank, qtok = mine.shape
    plen = parts[0].shape[2]
    return pl.pallas_call(
        functools.partial(collect_kernel, len(parts)),
        in_specs=[VMEM] * (len(parts) + 5),
        out_specs=VMEM,
        out_shape=jax.ShapeDtypeStruct((rank, 3 * plen + qtok + LANES), f32),
        compiler_params=pltpu.CompilerParams(vmem_limit_bytes=4 * 2**20),
        cost_estimate=cost(0.3),
        name="collect",
    )(*parts, mine, recv, r, r_p, up)


def grad_kernel(plen, qtok, info_ref, p_ref, q_ref, mine_ref, other_ref, out_ref):
    core = info_ref[2]
    width = p_ref.shape[1]
    queries = slice(2 * plen, 2 * plen + qtok)
    q_mine, q_other = mine_ref[:, queries].astype(bf16), other_ref[:, queries].astype(bf16)
    q_dlow = [jnp.where(core == i, q_mine, q_other) for i in range(2)]
    p_dlow = []
    for i in range(2):
        r = jnp.where(core == i, mine_ref[:, -plen:], other_ref[:, -plen:])
        rows = slice(i * plen, (i + 1) * plen)
        p_dlow.append(((mine_ref[:, rows] + other_ref[:, rows]) * r).astype(bf16))
    total = dot(jnp.concatenate(q_dlow, axis=1), q_ref[...], NN)
    total += dot(jnp.concatenate(p_dlow, axis=1), p_ref[...], NN)
    out_ref[:, :width] = total
    ups = slice(2 * plen + qtok, 2 * plen + qtok + LANES)
    out_ref[:, width:] = (mine_ref[:, ups] + other_ref[:, ups])


def grad_all(info, passage_rows, query_rows, mine, other, plen, qtok):
    rank, width = mine.shape[0], passage_rows.shape[1]
    return pl.pallas_call(
        functools.partial(grad_kernel, plen, qtok),
        in_specs=[SMEM] + [VMEM] * 4,
        out_specs=VMEM,
        out_shape=jax.ShapeDtypeStruct((rank, width + LANES), f32),
        compiler_params=pltpu.CompilerParams(vmem_limit_bytes=4 * 2**20),
        cost_estimate=cost(1.3),
        name="grad_all",
    )(info, passage_rows, query_rows, mine, other)


def swap(x):
    return lax.ppermute(x, "sub", [(0, 1), (1, 0)])


def across(x, nshard, step):
    return lax.ppermute(x, "shard", [(i, i ^ step) for i in range(nshard)])


def gather_packs(pack, nshard, groups):
    if nshard == 8:
        pack = pack[None]
        near = [pack] + [across(pack, nshard, k) for k in (2, 4, 6)]
        return near + [swap(piece) for piece in near], (0, 1, 2, 3)
    near = lax.all_gather(pack, "shard", axis_index_groups=groups)
    return [near, swap(near)], tuple(range(nshard // 2))


def exchange_parts(parts, steps, nshard, groups):
    if len(parts) == 1:
        parts = lax.all_to_all(parts[0], "shard", split_axis=0, concat_axis=0, tiled=True, axis_index_groups=groups)
        return [jnp.sum(parts.astype(f32), axis=0)]
    return [parts[0]] + [across(part, nshard, 2 * step) for part, step in reversed([*zip(parts, steps, strict=True)][1:])]


def power_of_two(exponent):
    power = jnp.ones_like(exponent)
    for sign in (1, -1):
        digits = jnp.maximum(sign * exponent, 0.0).astype(jnp.int32)
        for k in range(7):
            power = power * jnp.where((digits >> k) % 2 == 1, 2.0 ** (sign * 2**k), 1.0)
    return power


def coded(x):
    largest = jnp.max(jnp.abs(x), axis=1, keepdims=True)
    exponent = jnp.ceil(jnp.log2(jnp.clip(largest, 1e-20, 1e30))) - 14.0
    held = jnp.broadcast_to(exponent, (x.shape[0], LANES))
    scaled = jnp.concatenate([x * power_of_two(-exponent), held], axis=1)
    return scaled.astype(jnp.float16)


def decoded(x):
    x = x.astype(f32)
    return x[:, :-LANES] * power_of_two(x[:, -LANES : 1 - LANES])


def sum_over_shards(x, nshard, width):
    if nshard != 8:
        x = lax.psum(x, "shard")
        return x[:, :width], x[:, width:]
    x = coded(x)
    x = coded(decoded(x) + decoded(across(x, nshard, 1)))
    a, b, c = (decoded(across(x, nshard, k)) for k in (6, 4, 2))
    x = (decoded(x) + c) + (a + b)
    return x[:, :width], x[:, width:]


def per_device(
    query_hidden_states,
    passage_hidden_states,
    projection_matrix,
    adapter_down_weight,
    adapter_up_weight,
    passage_pair_index,
    passage_row_table,
):
    nshard = lax.axis_size("shard")
    core = lax.axis_index("sub").astype(jnp.int32)
    shard = lax.axis_index("shard").astype(jnp.int32)
    info = jnp.stack([shard % 2, shard // 2, core])
    groups = [list(range(parity, nshard, 2)) for parity in range(2)]
    qdev, qlen, width = query_hidden_states.shape
    pdev, plen, _ = passage_hidden_states.shape
    half = qdev // 2
    qtok = half * qlen
    query_rows = query_hidden_states.reshape(qdev * qlen, width)
    passage_rows = passage_hidden_states.reshape(pdev * plen, width)

    send_p, keep_p, query_vmem, weight = project_passages(
        info, passage_rows, query_rows, projection_matrix, jnp.transpose(adapter_down_weight)
    )
    send_q, keep_q = project_queries(query_vmem, weight, adapter_up_weight.shape[0])
    ppack, r_p = pack_passage(keep_p, swap(send_p), adapter_up_weight)
    mine, r_q = pack_queries(
        info, passage_row_table, jnp.transpose(passage_pair_index), keep_q, swap(send_q), adapter_up_weight
    )
    other = across(mine, nshard, 1)
    packs, steps = gather_packs(ppack, nshard, groups)

    stats, total, sums, weights, vqt = score_forward(packs, steps, info, mine, other, qlen, qtok, plen)
    *parts, dlow_mine, dlow_other, gup, loss = score_backward(
        packs,
        steps,
        info,
        mine,
        other,
        adapter_up_weight,
        stats,
        total,
        sums,
        across(sums, nshard, 1),
        weights,
        unit_of(packs, weights, qlen),
        vqt,
        qlen,
        qtok,
        plen,
    )
    parts = exchange_parts(parts, steps, nshard, groups)
    collected = collect(parts, dlow_mine, across(dlow_other, nshard, 1), r_q, r_p, gup)
    grads = grad_all(info, passage_rows, query_rows, collected, swap(collected), plen, qtok)
    loss, _ = lax.optimization_barrier((loss, grads))
    down_sum, up_sum = sum_over_shards(grads, nshard, width)
    query_loss = lax.dynamic_slice_in_dim(loss[0], info[0] * half, half, 0)
    return (query_loss, jnp.transpose(down_sum), up_sum)


def solution(mesh):
    placed = (
        P(("groups", "shard"), None, "sub"),
        P(("groups", "shard"), None, "sub"),
        P("sub", None),
        P("sub", None),
        P(),
        P(("groups", "shard"), None),
        P("groups"),
    )
    return jax.shard_map(
        per_device,
        mesh=mesh,
        in_specs=placed,
        out_specs=(P(("groups", "shard", "sub")), P(("groups", "sub"), None), P("groups", None)),
        check_vma=False,
    )
```

```python
import functools
import math

import jax
import jax.numpy as jnp
from jax import lax
from jax.experimental import pallas as pl
from jax.experimental.pallas import tpu as pltpu
from jax.sharding import PartitionSpec as P

pool_temp = 0.05
loss_temp = 0.05
norm_eps = 1e-06
bf16 = jnp.bfloat16
f32 = jnp.float32
LANES = 128
EXP_SCALE = math.log2(math.e) / pool_temp
VMEM = pl.BlockSpec(memory_space=pltpu.VMEM)
SMEM = pl.BlockSpec(memory_space=pltpu.SMEM)
HBM = pl.BlockSpec(memory_space=pltpu.HBM)


def cost(microseconds):
    return pl.CostEstimate(
        flops=int(microseconds * 1.1e9), bytes_accessed=int(microseconds * 3.5e6), transcendentals=0
    )


def dot(a, b, contract, precision=None):
    return lax.dot_general(
        a, b, ((contract[0], contract[1]), ((), ())), precision=precision, preferred_element_type=f32
    )


NN = ((1,), (0,))
NT = ((1,), (1,))
TN = ((0,), (0,))


def put_projection(send_ref, keep_ref, projected, rank):
    tokens = projected.shape[0] // 2
    low = jnp.transpose(projected[:, LANES:])[:rank, :]
    for i, ref in enumerate((send_ref, keep_ref)):
        ref[:tokens, :] = projected[i * tokens : (i + 1) * tokens, :LANES]
        for t in range(tokens // LANES):
            at = i * tokens + t * LANES
            ref[tokens + t * rank : tokens + (t + 1) * rank, :] = low[:, at : at + LANES]


def project_passages_kernel(
    info_ref, p_hbm, q_hbm, proj_hbm, down_hbm, send_ref, keep_ref, q_ref, weight_ref, p_ref, down_ref, sems
):
    core = info_ref[2]
    weights = [
        pltpu.make_async_copy(down_hbm, down_ref, sems.at[0]),
        pltpu.make_async_copy(proj_hbm, weight_ref.at[:, :LANES], sems.at[1]),
    ]
    loads = []
    for source, to in ((p_hbm, p_ref), (q_hbm, q_ref)):
        half = source.shape[0] // 2
        for i, owner in enumerate((1 - core, core)):
            rows = pl.ds(pl.multiple_of(owner * half, LANES), half)
            copy = pltpu.make_async_copy(
                source.at[rows, :], to.at[i * half : (i + 1) * half, :], sems.at[2 + len(loads)]
            )
            loads.append(copy)
    for copy in weights + loads[:2]:
        copy.start()
    weights[0].wait()
    rank, width = down_ref.shape
    low = jnp.concatenate([down_ref[...].astype(f32), jnp.zeros((LANES - rank, width), f32)], axis=0)
    weight_ref[:, LANES:] = jnp.transpose(low).astype(bf16)
    weights[1].wait()
    for copy in loads[2:]:
        copy.start()
    for copy in loads[:2]:
        copy.wait()
    put_projection(send_ref, keep_ref, dot(p_ref[...], weight_ref[...], NN), rank)
    for copy in loads[2:]:
        copy.wait()


def project_passages(info, passage_rows, query_rows, projection, down):
    half, width = passage_rows.shape[0] // 2, passage_rows.shape[1]
    rank = down.shape[0]
    shape = jax.ShapeDtypeStruct((half + half // LANES * rank, LANES), f32)
    operands = (passage_rows, query_rows, projection, down)
    operands = [pltpu.with_memory_space_constraint(x, pltpu.HBM) for x in operands]
    return pl.pallas_call(
        project_passages_kernel,
        in_specs=[SMEM] + [HBM] * 4,
        out_specs=[VMEM] * 4,
        out_shape=(
            shape,
            shape,
            pltpu.VMEM(query_rows.shape, bf16),
            pltpu.VMEM((width, 2 * LANES), bf16),
        ),
        scratch_shapes=[
            pltpu.VMEM((2 * half, width), bf16),
            pltpu.VMEM((rank, width), bf16),
            pltpu.SemaphoreType.DMA((6,)),
        ],
        compiler_params=pltpu.CompilerParams(vmem_limit_bytes=8 * 2**20),
        cost_estimate=cost(3.7),
        name="project_passages",
    )(info, *operands)


def project_queries_kernel(rank, q_ref, weight_ref, send_ref, keep_ref):
    put_projection(send_ref, keep_ref, dot(q_ref[...], weight_ref[...], NN), rank)


def project_queries(query_rows, weight, rank):
    half = query_rows.shape[0] // 2
    shape = jax.ShapeDtypeStruct((half + half // LANES * rank, LANES), f32)
    return pl.pallas_call(
        functools.partial(project_queries_kernel, rank),
        in_specs=[VMEM] * 2,
        out_specs=[VMEM] * 2,
        out_shape=(shape, shape),
        compiler_params=pltpu.CompilerParams(vmem_limit_bytes=4 * 2**20),
        cost_estimate=cost(1.5),
        name="project_queries",
    )(query_rows, weight)


def pad_lanes(x):
    return jnp.concatenate([x, jnp.zeros((x.shape[0], LANES - x.shape[1]), x.dtype)], axis=1)


def pack_rows(keep_ref, recv_ref, up, out_ref, r_ref):
    rank, tokens = up.shape[0], r_ref.shape[1]
    for t in range(tokens // LANES):
        block = slice(t * LANES, (t + 1) * LANES)
        rows = slice(tokens + t * rank, tokens + (t + 1) * rank)
        low = (keep_ref[rows, :] + recv_ref[rows, :]).astype(bf16)
        full = keep_ref[block, :] + recv_ref[block, :] + dot(low, up, TN)
        r = lax.rsqrt(jnp.sum(full * full, axis=1, keepdims=True) + norm_eps)
        out_ref[block, :] = (full * r).astype(bf16)
        r = jnp.transpose(jnp.broadcast_to(r, (LANES, LANES)))
        out_ref[rows, :] = (low.astype(f32) * r[:rank, :]).astype(bf16)
        r_ref[:, block] = r[:8, :]


def pack_passage_kernel(keep_ref, recv_ref, up_ref, out_ref, r_ref):
    pack_rows(keep_ref, recv_ref, up_ref[...], out_ref, r_ref)


def pack_passage(keep, recv, up):
    rank = up.shape[0]
    tokens = keep.shape[0] // (LANES + rank) * LANES
    return pl.pallas_call(
        pack_passage_kernel,
        in_specs=[VMEM] * 3,
        out_specs=[VMEM] * 2,
        out_shape=(
            jax.ShapeDtypeStruct((tokens + tokens // LANES * rank, LANES), bf16),
            jax.ShapeDtypeStruct((8, tokens), f32),
        ),
        compiler_params=pltpu.CompilerParams(vmem_limit_bytes=4 * 2**20),
        cost_estimate=cost(6),
        name="pack_passage",
    )(keep, recv, up)


def pack_queries_kernel(info_ref, table_ref, ids_ref, keep_ref, recv_ref, up_ref, out_ref, r_ref):
    pack_rows(keep_ref, recv_ref, up_ref[...], out_ref, r_ref)
    ids = ids_ref[...]
    cands, qdev = ids.shape
    n_ids = table_ref.shape[0]
    if n_ids <= 16:
        rows = jnp.zeros(ids.shape, jnp.int32)
        for i in range(n_ids):
            rows = jnp.where(ids == i, table_ref[i], rows)
    else:
        rows = lax.fori_loop(
            0, n_ids, lambda i, c: jnp.where(ids == i, table_ref[i], c), jnp.zeros(ids.shape, jnp.int32)
        )
    half = qdev // 2
    wide = jnp.concatenate([pad_lanes(rows.astype(f32)), jnp.full((16 - cands, LANES), -1.0, f32)], axis=0)
    place = info_ref[0] * half
    wide = pltpu.roll(wide, lax.rem(place - info_ref[2] * half + LANES, LANES), 1)
    lane = lax.broadcasted_iota(jnp.int32, wide.shape, 1)
    wide = jnp.where((lane >= place) & (lane < place + half), wide, -1.0)
    out_ref[out_ref.shape[0] - 16 :, :] = wide.astype(bf16)


def pack_queries(info, table, ids, keep, recv, up):
    rank = up.shape[0]
    tokens = keep.shape[0] // (LANES + rank) * LANES
    return pl.pallas_call(
        pack_queries_kernel,
        in_specs=[SMEM] * 2 + [VMEM] * 4,
        out_specs=[VMEM] * 2,
        out_shape=(
            jax.ShapeDtypeStruct((tokens + tokens // LANES * rank + 16, LANES), bf16),
            jax.ShapeDtypeStruct((8, tokens), f32),
        ),
        compiler_params=pltpu.CompilerParams(vmem_limit_bytes=4 * 2**20),
        cost_estimate=cost(0.9),
        name="pack_queries",
    )(info, table, ids, keep, recv, up)


def both_queries(lo, mine_ref, other_ref, at):
    mine, other = mine_ref[at, :], other_ref[at, :]
    return jnp.where(lo == 0, mine, other), jnp.where(lo == 0, other, mine)


def over_packs(packs, body):
    at = 0
    for pack in packs:
        n = pack.shape[0]
        if n <= 8:
            for p in range(n):
                body(pack, p, at + p)
        else:
            lax.fori_loop(0, n, lambda p, c, pack=pack, at=at: (body(pack, p, at + p), c)[1], 0)
        at += n


def same_query(shape, dim, qlen):
    token = lax.broadcasted_iota(jnp.int32, shape, dim) // qlen
    return (token == lax.broadcasted_iota(jnp.int32, shape, 1 - dim)).astype(bf16)


def parts_of(wide, n):
    parts = []
    for _ in range(n):
        parts.append(wide.astype(bf16))
        wide = wide - parts[-1].astype(f32)
    return parts


def expo_of(vp, vqt):
    return jnp.exp2(dot(vp, vqt, NN) * EXP_SCALE)


def forward_kernel(cfg, *refs):
    qlen, qtok, plen, store, where, n_packs = cfg
    packs = refs[:n_packs]
    info_ref, mine_ref, other_ref = refs[n_packs : n_packs + 3]
    stats_ref, total_ref, sums_ref, weights_ref, vqt_ref = refs[n_packs + 3 :]
    lo = info_ref[0]
    first_half, second_half = both_queries(lo, mine_ref, other_ref, slice(0, qtok))
    vqt_ref[:, :qtok] = jnp.transpose(first_half.astype(f32)).astype(bf16)
    vqt_ref[:, qtok:] = jnp.transpose(second_half.astype(f32)).astype(bf16)
    tail = slice(mine_ref.shape[0] - 16, mine_ref.shape[0])
    rows = jnp.maximum(mine_ref[tail, :].astype(f32), other_ref[tail, :].astype(f32))

    def forward(pack, p, pos):
        expo = expo_of(pack[p, :plen, :], vqt_ref[...])
        total = jnp.sum(expo, axis=0, keepdims=True)
        total_ref[pl.ds(pos, 1), :] = total
        if store:
            weights_ref[pos] = (expo * (1.0 / total)).astype(bf16)
        hi, core = where(info_ref, pos)
        here = (rows == ((hi * 2 + lo) * 2 + core).astype(f32)).astype(f32)
        stats_ref[1, pl.ds(pos, 1), :] = jnp.sum(here, axis=0, keepdims=True)
        stats_ref[2, pl.ds(pos, 1), :] = here[:1, :]

    over_packs(packs, forward)
    same = same_query((2 * qtok, LANES), 0, qlen)
    logits = sum(dot(part, same, NN) for part in parts_of(jnp.log(total_ref[...]), 3)) * (1.0 / qlen)
    stats_ref[0] = logits
    sums_ref[...] = jnp.zeros_like(sums_ref)
    sums_ref[:1, :] = jnp.sum(stats_ref[1] * jnp.exp(logits), axis=0, keepdims=True)
    sums_ref[1:2, :] = jnp.sum(stats_ref[2] * logits, axis=0, keepdims=True)


def backward_kernel(cfg, *refs):
    qlen, qtok, plen, store, where, n_packs = cfg
    packs = refs[:n_packs]
    info_ref, mine_ref, other_ref, up_ref, stats_ref, total_ref, sums_ref, recv_ref = refs[n_packs : n_packs + 8]
    weights_ref, unit_ref, vqt_ref = refs[n_packs + 8 : n_packs + 11]
    refs = refs[n_packs + 11 :]
    n_parts = n_packs // 2 if store else 1
    part_refs, (dmine_ref, dother_ref, gup_ref, loss_ref) = refs[:n_parts], refs[n_parts : n_parts + 4]
    scale_ref, dvqt_ref, grad_ref, dv_ref, dvb_ref = refs[n_parts + 4 :]
    up = up_ref[...]
    rank = up.shape[0]
    lo = info_ref[0]
    vq = jnp.concatenate(both_queries(lo, mine_ref, other_ref, slice(0, qtok)), axis=0)
    logits, mult, first = stats_ref[0], stats_ref[1], stats_ref[2]
    summed = sums_ref[:1, :] + recv_ref[:1, :]
    live = lax.broadcasted_iota(jnp.int32, summed.shape, 1) < 2 * qtok // qlen
    summed = jnp.where(live, summed, 1.0)
    loss_ref[...] = jnp.broadcast_to(jnp.log(summed) - (sums_ref[1:2, :] + recv_ref[1:2, :]), loss_ref.shape)
    dscore = (mult * jnp.exp(logits) / summed - first) * (1.0 / loss_temp)
    same = same_query((LANES, 2 * qtok), 1, qlen)
    scale_ref[...] = sum(dot(part, same, NN) for part in parts_of(dscore, 3))

    def scaled_low(pack, p):
        blocks = range(plen, plen + plen // LANES * rank, rank)
        return jnp.concatenate([pack[p, at : at + rank, :] for at in blocks], axis=1)

    def project_out(vp, dv):
        vpf = vp.astype(f32)
        return parts_of(dv - vpf * jnp.sum(vpf * dv, axis=1, keepdims=True), 2)

    if store:
        for pos in range(n_packs):
            rows = slice(pos * plen, (pos + 1) * plen)
            grad_ref[rows, :] = (weights_ref[pos].astype(f32) * (scale_ref[pos : pos + 1, :] * (1.0 / qlen))).astype(bf16)
            dv_ref[rows, :] = dot(grad_ref[rows, :], vq, NN)
            dvqt = unit_ref[pos].astype(f32) * scale_ref[pos : pos + 1, :]
            dvqt_ref[...] = dvqt if pos == 0 else dvqt_ref[...] + dvqt
        for pos, pack in enumerate(packs):
            rows = slice(pos * plen, (pos + 1) * plen)
            dv = project_out(pack[0, :plen, :], dv_ref[rows, :])
            dvb_ref[0, rows, :], dvb_ref[1, rows, :] = dv
            part_refs[pos % n_parts][where(info_ref, pos)[1]] = (dot(up, dv[0], NT) + dot(up, dv[1], NT))
        lows = jnp.concatenate([scaled_low(pack, 0) for pack in packs], axis=1)
        gup = dot(lows, dvb_ref[0], NN) + dot(lows, dvb_ref[1], NN)
    else:
        dvqt_ref[...] = jnp.zeros_like(dvqt_ref)
        gup_ref[...] = jnp.zeros_like(gup_ref)

        def backward(pack, p, pos):
            vp = pack[p, :plen, :]
            scale = scale_ref[pl.ds(pos, 1), :]
            weights = (expo_of(vp, vqt_ref[...]) * (1.0 / total_ref[pl.ds(pos, 1), :])).astype(bf16)
            unit = (dot(vp, weights, TN) * (1.0 / qlen)).astype(bf16)
            dvqt_ref[...] += unit.astype(f32) * scale
            grad = (weights.astype(f32) * (scale * (1.0 / qlen))).astype(bf16)
            dv = project_out(vp, dot(grad, vq, NN))
            hi, core = where(info_ref, pos)
            part_refs[0][hi, core] = (dot(up, dv[0], NT) + dot(up, dv[1], NT))
            low = scaled_low(pack, p)
            gup_ref[...] += dot(low, dv[0], NN) + dot(low, dv[1], NN)

        over_packs(packs, backward)
        gup = gup_ref[...]

    vqt = vqt_ref[...].astype(f32)
    dvqt = dvqt_ref[...]
    dvqt = parts_of(dvqt - vqt * jnp.sum(vqt * dvqt, axis=0, keepdims=True), 2)
    dlow = dot(up, dvqt[0], NN) + dot(up, dvqt[1], NN)
    dmine_ref[...] = jnp.where(lo == 0, dlow[:, :qtok], dlow[:, qtok:])
    dother_ref[...] = jnp.where(lo == 0, dlow[:, qtok:], dlow[:, :qtok])
    lows = [
        both_queries(lo, mine_ref, other_ref, slice(at, at + rank))
        for at in range(qtok, qtok + qtok // LANES * rank, rank)
    ]
    lows = jnp.concatenate([low[0] for low in lows] + [low[1] for low in lows], axis=1)
    gup_ref[...] = gup + dot(lows, dvqt[0], NT) + dot(lows, dvqt[1], NT)


def places(steps):
    def where(info_ref, pos):
        n = len(steps)
        if n == 4:
            return jnp.bitwise_xor(info_ref[1], steps[pos % n]), info_ref[2] if pos < n else 1 - info_ref[2]
        return lax.rem(pos, n), jnp.where(pos < n, info_ref[2], 1 - info_ref[2])

    return where


def score_forward(packs, steps, info, mine, other, qlen, qtok, plen):
    npos = 2 * len(steps)
    store = len(packs) == npos
    cfg = (qlen, qtok, plen, store, places(steps), len(packs))
    return pl.pallas_call(
        functools.partial(forward_kernel, cfg),
        in_specs=[VMEM] * len(packs) + [SMEM] + [VMEM] * 2,
        out_specs=[VMEM] * 5,
        out_shape=(
            jax.ShapeDtypeStruct((3, npos, LANES), f32),
            jax.ShapeDtypeStruct((npos, 2 * qtok), f32),
            jax.ShapeDtypeStruct((8, LANES), f32),
            jax.ShapeDtypeStruct((npos, plen, 2 * qtok) if store else (1, 16, LANES), bf16),
            jax.ShapeDtypeStruct((LANES, 2 * qtok), bf16),
        ),
        compiler_params=pltpu.CompilerParams(vmem_limit_bytes=(16 if store else 40) * 2**20),
        cost_estimate=cost(1.9),
        name="score_forward",
    )(*packs, info, mine, other)


def unit_kernel(qlen, plen, *refs):
    packs, (weights_ref, unit_ref) = refs[:-2], refs[-2:]
    for pos, pack in enumerate(packs):
        unit_ref[pos] = (dot(pack[0, :plen, :], weights_ref[pos], TN) * (1.0 / qlen)).astype(bf16)


def unit_of(packs, weights, qlen):
    npos, plen, ntok = weights.shape
    if npos != len(packs):
        return jnp.zeros((1, 16, LANES), bf16)
    return pl.pallas_call(
        functools.partial(unit_kernel, qlen, plen),
        in_specs=[VMEM] * (npos + 1),
        out_specs=VMEM,
        out_shape=jax.ShapeDtypeStruct((npos, LANES, ntok), bf16),
        compiler_params=pltpu.CompilerParams(vmem_limit_bytes=4 * 2**20),
        cost_estimate=cost(1.2),
        name="unit",
    )(*packs, weights)


def score_backward(packs, steps, info, mine, other, up, stats, total, sums, recv, weights, unit, vqt, qlen, qtok, plen):
    npos, rank = 2 * len(steps), up.shape[0]
    store = len(packs) == npos
    cfg = (qlen, qtok, plen, store, places(steps), len(packs))
    part = jax.ShapeDtypeStruct((2, rank, plen), f32)
    whole = jax.ShapeDtypeStruct((len(steps), 2, rank, plen), f32)
    kept = npos * plen if store else 16
    parts = (part,) * len(steps) if store else (whole,)
    return pl.pallas_call(
        functools.partial(backward_kernel, cfg),
        in_specs=[VMEM] * len(packs) + [SMEM] + [VMEM] * 10,
        out_specs=[VMEM] * (len(parts) + 4),
        out_shape=(
            *parts,
            jax.ShapeDtypeStruct((rank, qtok), f32),
            jax.ShapeDtypeStruct((rank, qtok), f32),
            jax.ShapeDtypeStruct((rank, LANES), f32),
            jax.ShapeDtypeStruct((8, LANES), f32),
        ),
        scratch_shapes=[
            pltpu.VMEM((npos, 2 * qtok), f32),
            pltpu.VMEM((LANES, 2 * qtok), f32),
            pltpu.VMEM((kept, 2 * qtok), bf16),
            pltpu.VMEM((kept, LANES), f32),
            pltpu.VMEM((2, kept, LANES), bf16),
        ],
        compiler_params=pltpu.CompilerParams(vmem_limit_bytes=(20 if store else 40) * 2**20),
        cost_estimate=cost(2.5),
        name="score_backward",
    )(*packs, info, mine, other, up, stats, total, sums, recv, weights, unit, vqt)


def collect_kernel(n, *refs):
    parts, (mine_ref, recv_ref, r_ref, r_p_ref, up_ref, out_ref) = refs[:n], refs[n:]
    _, _, plen = parts[0].shape
    qtok = mine_ref.shape[1]
    for i in range(2):
        out_ref[:, i * plen : (i + 1) * plen] = sum(part[i].astype(f32) for part in parts)
    out_ref[:, 2 * plen : 2 * plen + qtok] = (mine_ref[...] + recv_ref[...].astype(f32)) * r_ref[:1, :]
    out_ref[:, 2 * plen + qtok : 2 * plen + qtok + LANES] = up_ref[...]
    out_ref[:, 2 * plen + qtok + LANES :] = jnp.broadcast_to(r_p_ref[:1, :], (out_ref.shape[0], plen))


def collect(parts, mine, recv, r, r_p, up):
    rank, qtok = mine.shape
    plen = parts[0].shape[2]
    return pl.pallas_call(
        functools.partial(collect_kernel, len(parts)),
        in_specs=[VMEM] * (len(parts) + 5),
        out_specs=VMEM,
        out_shape=jax.ShapeDtypeStruct((rank, 3 * plen + qtok + LANES), f32),
        compiler_params=pltpu.CompilerParams(vmem_limit_bytes=4 * 2**20),
        cost_estimate=cost(0.3),
        name="collect",
    )(*parts, mine, recv, r, r_p, up)


def grad_kernel(plen, qtok, info_ref, p_ref, q_ref, mine_ref, other_ref, out_ref):
    core = info_ref[2]
    width = p_ref.shape[1]
    queries = slice(2 * plen, 2 * plen + qtok)
    q_mine, q_other = mine_ref[:, queries].astype(bf16), other_ref[:, queries].astype(bf16)
    q_dlow = [jnp.where(core == i, q_mine, q_other) for i in range(2)]
    p_dlow = []
    for i in range(2):
        r = jnp.where(core == i, mine_ref[:, -plen:], other_ref[:, -plen:])
        rows = slice(i * plen, (i + 1) * plen)
        p_dlow.append(((mine_ref[:, rows] + other_ref[:, rows]) * r).astype(bf16))
    total = dot(jnp.concatenate(q_dlow, axis=1), q_ref[...], NN)
    total += dot(jnp.concatenate(p_dlow, axis=1), p_ref[...], NN)
    out_ref[:, :width] = total
    ups = slice(2 * plen + qtok, 2 * plen + qtok + LANES)
    out_ref[:, width:] = (mine_ref[:, ups] + other_ref[:, ups])


def grad_all(info, passage_rows, query_rows, mine, other, plen, qtok):
    rank, width = mine.shape[0], passage_rows.shape[1]
    return pl.pallas_call(
        functools.partial(grad_kernel, plen, qtok),
        in_specs=[SMEM] + [VMEM] * 4,
        out_specs=VMEM,
        out_shape=jax.ShapeDtypeStruct((rank, width + LANES), f32),
        compiler_params=pltpu.CompilerParams(vmem_limit_bytes=4 * 2**20),
        cost_estimate=cost(1.3),
        name="grad_all",
    )(info, passage_rows, query_rows, mine, other)


def swap(x):
    return lax.ppermute(x, "sub", [(0, 1), (1, 0)])


def across(x, nshard, step):
    return lax.ppermute(x, "shard", [(i, i ^ step) for i in range(nshard)])


def gather_packs(pack, nshard, groups):
    if nshard == 8:
        pack = pack[None]
        near = [pack] + [across(pack, nshard, k) for k in (2, 4, 6)]
        return near + [swap(piece) for piece in near], (0, 1, 2, 3)
    near = lax.all_gather(pack, "shard", axis_index_groups=groups)
    return [near, swap(near)], tuple(range(nshard // 2))


def exchange_parts(parts, steps, nshard, groups):
    if len(parts) == 1:
        parts = lax.all_to_all(parts[0], "shard", split_axis=0, concat_axis=0, tiled=True, axis_index_groups=groups)
        return [jnp.sum(parts.astype(f32), axis=0)]
    return [parts[0]] + [across(part, nshard, 2 * step) for part, step in reversed([*zip(parts, steps, strict=True)][1:])]


def power_of_two(exponent):
    power = jnp.ones_like(exponent)
    for sign in (1, -1):
        digits = jnp.maximum(sign * exponent, 0.0).astype(jnp.int32)
        for k in range(7):
            power = power * jnp.where((digits >> k) % 2 == 1, 2.0 ** (sign * 2**k), 1.0)
    return power


def coded(x):
    largest = jnp.max(jnp.abs(x), axis=1, keepdims=True)
    exponent = jnp.ceil(jnp.log2(jnp.clip(largest, 1e-20, 1e30))) - 14.0
    held = jnp.broadcast_to(exponent, (x.shape[0], LANES))
    scaled = jnp.concatenate([x * power_of_two(-exponent), held], axis=1)
    return scaled.astype(jnp.float16)


def decoded(x, columns=slice(0, -LANES)):
    return x[:, columns].astype(f32) * power_of_two(x[:, -LANES : 1 - LANES].astype(f32))


def sum_over_shards(x, nshard, width):
    if nshard != 8:
        x = lax.psum(x, "shard")
        return x[:, :width], x[:, width:]
    x = coded(x)
    x = coded(decoded(x) + decoded(across(x, nshard, 1)))
    arrays = [x] + [across(x, nshard, k) for k in (6, 4, 2)]

    def total(columns):
        x, a, b, c = (decoded(array, columns) for array in arrays)
        return (x + c) + (a + b)

    return total(slice(0, width)), total(slice(width, -LANES))


def per_device(
    query_hidden_states,
    passage_hidden_states,
    projection_matrix,
    adapter_down_weight,
    adapter_up_weight,
    passage_pair_index,
    passage_row_table,
):
    nshard = lax.axis_size("shard")
    core = lax.axis_index("sub").astype(jnp.int32)
    shard = lax.axis_index("shard").astype(jnp.int32)
    info = jnp.stack([shard % 2, shard // 2, core])
    groups = [list(range(parity, nshard, 2)) for parity in range(2)]
    qdev, qlen, width = query_hidden_states.shape
    pdev, plen, _ = passage_hidden_states.shape
    half = qdev // 2
    qtok = half * qlen
    query_rows = query_hidden_states.reshape(qdev * qlen, width)
    passage_rows = passage_hidden_states.reshape(pdev * plen, width)

    send_p, keep_p, query_vmem, weight = project_passages(
        info, passage_rows, query_rows, projection_matrix, jnp.transpose(adapter_down_weight)
    )
    send_q, keep_q = project_queries(query_vmem, weight, adapter_up_weight.shape[0])
    ppack, r_p = pack_passage(keep_p, swap(send_p), adapter_up_weight)
    mine, r_q = pack_queries(
        info, passage_row_table, jnp.transpose(passage_pair_index), keep_q, swap(send_q), adapter_up_weight
    )
    other = across(mine, nshard, 1)
    packs, steps = gather_packs(ppack, nshard, groups)

    stats, total, sums, weights, vqt = score_forward(packs, steps, info, mine, other, qlen, qtok, plen)
    *parts, dlow_mine, dlow_other, gup, loss = score_backward(
        packs,
        steps,
        info,
        mine,
        other,
        adapter_up_weight,
        stats,
        total,
        sums,
        across(sums, nshard, 1),
        weights,
        unit_of(packs, weights, qlen),
        vqt,
        qlen,
        qtok,
        plen,
    )
    parts = exchange_parts(parts, steps, nshard, groups)
    collected = collect(parts, dlow_mine, across(dlow_other, nshard, 1), r_q, r_p, gup)
    grads = grad_all(info, passage_rows, query_rows, collected, swap(collected), plen, qtok)
    loss, _ = lax.optimization_barrier((loss, grads))
    down_sum, up_sum = sum_over_shards(grads, nshard, width)
    query_loss = lax.dynamic_slice_in_dim(loss[0], info[0] * half, half, 0)
    return (query_loss, jnp.transpose(down_sum), up_sum)


def solution(mesh):
    placed = (
        P(("groups", "shard"), None, "sub"),
        P(("groups", "shard"), None, "sub"),
        P("sub", None),
        P("sub", None),
        P(),
        P(("groups", "shard"), None),
        P("groups"),
    )
    return jax.shard_map(
        per_device,
        mesh=mesh,
        in_specs=placed,
        out_specs=(P(("groups", "shard", "sub")), P(("groups", "sub"), None), P("groups", None)),
        check_vma=False,
    )
```
